256 devices in a mesh: dp: 4 (over y_lo, core), lon: 16 (over y_hi, z), lat: 4 (over x).
Axes of the slice: x: 4, y: 4 (y_hi: 2, y_lo: 2; y = y_hi * 2 + y_lo), z: 8, core: 2. Of those that a mesh axis runs over, the one named last changes fastest.
Arguments:
- weather: bfloat16 [4, 8, 24, 384, 192], P('dp', None, 'lat', 'lon'), may hold values from -6 to 6
- cotangent: bfloat16 [4, 8, 24, 384, 192], P('dp', None, 'lat', 'lon'), may hold values from -6 to 6
- norm_gain: float32 [192], replicated, may hold values from 0.1 to 1.9
- qkv_weight: bfloat16 [192, 576], replicated, may hold values from -0.4375 to 0.4375
- proj_weight: bfloat16 [192, 192], replicated, may hold values from -0.4375 to 0.4375
- bias_table: float32 [4, 4, 6, 3312], P(None, 'lat'), may hold values from -3 to 281
Outputs:
- updated: bfloat16 [4, 8, 24, 384, 192], P('dp', None, 'lat', 'lon')
- grad_weather: bfloat16 [4, 8, 24, 384, 192], P('dp', None, 'lat', 'lon')
- grad_qkv: float32 [192, 576], replicated
- grad_proj: float32 [192, 192], replicated
- grad_gain: float32 [192], replicated
- grad_bias: float32 [4, 4, 6, 3312], P(None, 'lat')
The draws below stay inside these ranges and needn't reach their ends.
All inputs are finite; a program needn't handle non-finite values.
Results may differ from the reference program's by a relative error of at most 0.01.
Values may be sent and summed in bfloat16 or wider, within the bound.
No kernel may reach another device: no remote copies, remote signals or barrier semaphores. Data moves between devices by JAX's collectives and lax.ppermute only.
A program may use at most 192 MiB of HBM per device.

```python
import jax
import jax.numpy as jnp
from jax import lax

C = 192
HEADS = 6
WLEV = 2
WLAT = 6
WLON = 12
NLEV = 8
HD = 32
SHIFT_LEV = 1
SHIFT_LAT = 3
SHIFT_LON = 6
BIASN = 3312
BATCH = 4
NLAT = 24
NLON = 384
LEVW = 4
LATW = 4


def draw_bias_table(key, part):
    key = jax.random.fold_in(key, 7)
    table_shape = (LEVW, LATW, HEADS, BIASN)
    background_key = jax.random.fold_in(key, 0)
    values = jnp.clip(jax.random.normal(background_key, table_shape, jnp.float32), -3.0, 3.0)
    return values.astype(jnp.float32)


def shard_levels(stream_key, shape, cuts, least, top_value):
    gain, own = 1.0, jax.random.fold_in(stream_key, 6)
    for dim, shards_of in cuts:
        heights = jnp.exp(jax.random.uniform(jax.random.fold_in(own, dim), (shards_of,), jnp.float32, least / len(cuts), top_value / len(cuts)))
        gain = gain * jnp.repeat(heights, shape[dim] // shards_of).reshape([-1 if axis == dim else 1 for axis in range(len(shape))])
    return gain


def noise(rng, extent, spread, limit, pieces=(), kind=jnp.bfloat16):
    values = jax.random.normal(rng, extent, jnp.float32) * spread
    if len(pieces) > 0:
        values = shard_levels(rng, extent, pieces, -0.22, 0.18) * values
    return jnp.clip(values, min=-limit, max=limit).astype(kind)


def setup_inputs(seed: int = 0) -> dict:
    key_list = jax.random.split(jax.random.key(seed), 7)
    weather = noise(key_list[0], (BATCH, NLEV, NLAT, NLON, C), 1.0, 6.0, ((0, 4), (2, 4), (3, 16)))
    cotangent = noise(key_list[1], (BATCH, NLEV, NLAT, NLON, C), 1.0, 6.0, ((0, 4), (2, 4), (3, 16)))
    norm_gain = jnp.clip(1.0 + 0.18 * jax.random.normal(key_list[2], (C,), jnp.float32), 0.1, 1.9)
    qkv_weight = noise(key_list[3], (C, 3 * C), C ** -0.5, 0.4375)
    proj_weight = noise(key_list[4], (C, C), C ** -0.5, 0.4375)
    bias_table = draw_bias_table(jax.random.fold_in(key_list[6], 71), 0)
    return dict(weather=weather, cotangent=cotangent, norm_gain=norm_gain, qkv_weight=qkv_weight, proj_weight=proj_weight, bias_table=bias_table)


MASKED = -1e+30
EPSILON = 1e-05

def to_windows(values):
    samples, levels, rows_here, cols_here, channels = values.shape
    shaped = values.reshape(samples, levels // WLEV, WLEV, rows_here // WLAT, WLAT, cols_here // WLON, WLON, channels)
    shaped = shaped.transpose(1, 0, 3, 5, 2, 4, 6, 7)
    return shaped.reshape(levels // WLEV, samples, rows_here // WLAT, cols_here // WLON, WLEV * WLAT * WLON, channels)

def from_windows(blocks, samples, levels, rows_here, cols_here):
    channels = blocks.shape[-1]
    shaped = blocks.reshape(levels // WLEV, samples, rows_here // WLAT, cols_here // WLON, WLEV, WLAT, WLON, channels)
    shaped = shaped.transpose(1, 0, 4, 2, 5, 3, 6, 7)
    return shaped.reshape(samples, levels, rows_here, cols_here, channels)

def make_picker():
    lon_span = 2 * WLON - 1
    offsets = jnp.arange(WLON, dtype=jnp.int32)
    targets = jnp.arange(lon_span, dtype=jnp.int32)
    differ = offsets[None, :, None] - offsets[None, None, :] + WLON - 1
    return (differ == targets[:, None, None]).astype(jnp.float32)

def expand_bias(bias_table, picker):
    lev_windows, lat_windows, head_count, entries = bias_table.shape
    shaped = bias_table.reshape(lev_windows, lat_windows, head_count, WLEV, WLEV, WLAT, WLAT, 2 * WLON - 1)
    full = jnp.einsum('lahzyuvd,dxw->lahzuxyvw', shaped, picker, precision=lax.Precision.HIGHEST)
    window_size = WLEV * WLAT * WLON
    return full.reshape(lev_windows, lat_windows, head_count, window_size, window_size)

def fold_bias(score_sums, picker):
    lev_windows, lat_windows, head_count, window_size, other_size = score_sums.shape
    shaped = score_sums.reshape(lev_windows, lat_windows, head_count, WLEV, WLAT, WLON, WLEV, WLAT, WLON)
    folded = jnp.einsum('lahzuxyvw,dxw->lahzyuvd', shaped, picker, precision=lax.Precision.HIGHEST)
    return folded.reshape(lev_windows, lat_windows, head_count, WLEV * WLEV * WLAT * WLAT * (2 * WLON - 1))

def attend(operands):
    queries, key_rows, value_rows, grad_rows, bias_full, label_rows = operands
    leading = queries.shape[:-1]
    split_query = queries.astype(jnp.float32).reshape(leading + (HEADS, HD))
    split_key = key_rows.astype(jnp.float32).reshape(leading + (HEADS, HD))
    split_value = value_rows.astype(jnp.float32).reshape(leading + (HEADS, HD))
    split_grad = grad_rows.astype(jnp.float32).reshape(leading + (HEADS, HD))
    scores = jnp.einsum('maxihd,maxjhd->maxhij', split_query, split_key)
    scores = scores + bias_full[None, :, None]
    allowed = (label_rows[:, :, :, None] == label_rows[:, :, None, :])[None, :, :, None]
    scores = jnp.where(allowed, scores, MASKED)
    highest = lax.optimization_barrier(jnp.max(scores, axis=-1, keepdims=True))
    exponent = jnp.exp(scores - highest)
    probs = (exponent / lax.optimization_barrier(jnp.sum(exponent, axis=-1, keepdims=True))).astype(jnp.bfloat16)
    prob_float = probs.astype(jnp.float32)
    attended = jnp.einsum('maxhij,maxjhd->maxihd', prob_float, split_value).astype(jnp.bfloat16)
    grad_probs = jnp.einsum('maxihd,maxjhd->maxhij', split_grad, split_value)
    grad_value = jnp.einsum('maxhij,maxihd->maxjhd', prob_float, split_grad).astype(jnp.bfloat16)
    grad_scores = prob_float * (grad_probs - lax.optimization_barrier(jnp.sum(prob_float * grad_probs, axis=-1, keepdims=True)))
    score_sums = lax.optimization_barrier(jnp.sum(grad_scores, axis=(0, 2)))
    score_round = grad_scores.astype(jnp.bfloat16).astype(jnp.float32)
    inv_root = HD ** (-0.5)
    grad_query = (jnp.einsum('maxhij,maxjhd->maxihd', score_round, split_key) * inv_root).astype(jnp.bfloat16)
    grad_key = jnp.einsum('maxhij,maxihd->maxjhd', score_round, split_query).astype(jnp.bfloat16)
    width = HEADS * HD
    return (attended.reshape(leading + (width,)), grad_query.reshape(leading + (width,)), grad_key.reshape(leading + (width,)), grad_value.reshape(leading + (width,)), score_sums)

def local_pass(shifted, grad_shifted, norm_gain, qkv_weight, proj_weight, bias_full, group_rows):
    samples, levels, rows_here, cols_here, channels = shifted.shape
    dims = (samples, levels, rows_here, cols_here, channels)
    widened = shifted.astype(jnp.float32)
    centre = lax.optimization_barrier(jnp.mean(widened, axis=-1, keepdims=True))
    centred = widened - centre
    inv_std = lax.rsqrt(lax.optimization_barrier(jnp.mean(centred * centred, axis=-1, keepdims=True)) + EPSILON)
    normed = (centred * inv_std).reshape(-1, channels)
    inv_std = inv_std.reshape(-1, 1)
    hidden = (normed * norm_gain).astype(jnp.bfloat16)
    mixed = jnp.dot(hidden, qkv_weight, preferred_element_type=jnp.float32)
    inv_root = HD ** (-0.5)
    queries = (mixed[:, :channels] * inv_root).astype(jnp.bfloat16)
    key_flat = mixed[:, channels:2 * channels].astype(jnp.bfloat16)
    value_flat = mixed[:, 2 * channels:].astype(jnp.bfloat16)
    grad_flat = grad_shifted.reshape(-1, channels)
    grad_attended = jnp.dot(grad_flat, proj_weight.T, preferred_element_type=jnp.float32).astype(jnp.bfloat16)
    query_win = to_windows(queries.reshape(dims))
    key_win = to_windows(key_flat.reshape(dims))
    value_win = to_windows(value_flat.reshape(dims))
    grad_win = to_windows(grad_attended.reshape(dims))
    results = lax.map(attend, (query_win, key_win, value_win, grad_win, bias_full, group_rows))
    attended = from_windows(results[0], samples, levels, rows_here, cols_here).reshape(-1, channels)
    grad_query = from_windows(results[1], samples, levels, rows_here, cols_here).reshape(-1, channels)
    grad_key = from_windows(results[2], samples, levels, rows_here, cols_here).reshape(-1, channels)
    grad_value = from_windows(results[3], samples, levels, rows_here, cols_here).reshape(-1, channels)
    grad_mixed = jnp.concatenate([grad_query, grad_key, grad_value], axis=1)
    branch = jnp.dot(attended, proj_weight, preferred_element_type=jnp.float32).astype(jnp.bfloat16).reshape(dims)
    grad_proj = jnp.dot(attended.T, grad_flat, preferred_element_type=jnp.float32)
    grad_qkv = jnp.dot(hidden.T, grad_mixed, preferred_element_type=jnp.float32)
    grad_hidden = jnp.dot(grad_mixed, qkv_weight.T, preferred_element_type=jnp.float32)
    grad_gain = lax.optimization_barrier(jnp.sum(grad_hidden * normed, axis=0))
    grad_norm = grad_hidden * norm_gain
    grad_input = inv_std * (grad_norm - lax.optimization_barrier(jnp.mean(grad_norm, axis=-1, keepdims=True)) - normed * lax.optimization_barrier(jnp.mean(grad_norm * normed, axis=-1, keepdims=True)))
    grad_input = grad_input.astype(jnp.bfloat16).reshape(dims)
    return (branch, grad_input, grad_qkv, grad_proj, grad_gain, results[4])

def reference(weather, cotangent, norm_gain, qkv_weight, proj_weight, bias_table):
    batch, levels, rows_all, cols_all, channels = weather.shape
    level_region = (jnp.arange(levels, dtype=jnp.int32) >= levels - SHIFT_LEV).astype(jnp.int32)
    row_region = (jnp.arange(rows_all, dtype=jnp.int32) >= rows_all - SHIFT_LAT).astype(jnp.int32)
    groups = level_region[:, None, None] + 2 * row_region[None, :, None]
    groups = jnp.broadcast_to(groups, (levels, rows_all, cols_all))
    group_rows = to_windows(groups[None, :, :, :, None])[:, 0, :, :, :, 0]
    picker = make_picker()
    bias_full = expand_bias(bias_table, picker)
    forward_shift = (-SHIFT_LEV, -SHIFT_LAT, -SHIFT_LON)
    backward_shift = (SHIFT_LEV, SHIFT_LAT, SHIFT_LON)

    def one_sample(operands):
        weather_one, grad_one = operands
        shifted = jnp.roll(weather_one, forward_shift, axis=(1, 2, 3))
        grad_shifted = jnp.roll(grad_one, forward_shift, axis=(1, 2, 3))
        return local_pass(shifted, grad_shifted, norm_gain, qkv_weight, proj_weight, bias_full, group_rows)
    results = lax.map(one_sample, (weather[:, None], cotangent[:, None]))
    branch = results[0].reshape(weather.shape)
    grad_input = results[1].reshape(weather.shape)
    updated = (weather.astype(jnp.float32) + jnp.roll(branch, backward_shift, axis=(1, 2, 3)).astype(jnp.float32)).astype(jnp.bfloat16)
    grad_weather = (cotangent.astype(jnp.float32) + jnp.roll(grad_input, backward_shift, axis=(1, 2, 3)).astype(jnp.float32)).astype(jnp.bfloat16)
    factor = (batch * levels * rows_all * cols_all) ** (-0.5)
    grad_qkv = lax.optimization_barrier(jnp.sum(results[2], axis=0)) * factor
    grad_proj = lax.optimization_barrier(jnp.sum(results[3], axis=0)) * factor
    grad_gain = lax.optimization_barrier(jnp.sum(results[4], axis=0)) * factor
    grad_bias = fold_bias(lax.optimization_barrier(jnp.sum(results[5], axis=0)), picker) * factor
    return (updated, grad_weather, grad_qkv, grad_proj, grad_gain, grad_bias)
```

```python
import functools

import numpy as np
import jax
import jax.numpy as jnp
from jax import lax
from jax.experimental import pallas as pl
from jax.experimental.pallas import tpu as pltpu
from jax.sharding import PartitionSpec as P

HEADS = 6
WLEV = 2
WLAT = 6
WLON = 12
HD = 32
CH = 192
TOK = 144
LANES = 128
SHIFT_LAT = 3
SHIFT_LON = 6
SPAN = 2 * WLON - 1
GROUPS = WLEV * WLAT
MASKED = -1e30
EPSILON = 1e-05
BF = jnp.bfloat16
F32 = jnp.float32
PAY = 2048
WTILES = 6
BIAS_ROWS = 288
BROW = WTILES * CH
GROW = BROW + 3 * BIAS_ROWS
PIECE = 32
VMEM_LIMIT = 56 * 1024 * 1024


def place(rows, cols):
    return np.zeros((rows, cols), np.float32)


def gather_matrices(cols_here):
    windows = cols_here // WLON
    own_cols = cols_here - SHIFT_LON
    own = place(windows * WLAT * WLON, WLAT * cols_here)
    lat = place(windows * WLAT * WLON, SHIFT_LAT * own_cols)
    corner = place(windows * WLAT * WLON, WLAT * SHIFT_LON)
    for n in range(windows):
        for a in range(WLAT):
            for x in range(WLON):
                row = (n * WLAT + a) * WLON + x
                col = n * WLON + x
                if col < own_cols:
                    if a < SHIFT_LAT:
                        own[row, (a + SHIFT_LAT) * cols_here + col + SHIFT_LON] = 1
                    else:
                        lat[row, (a - SHIFT_LAT) * own_cols + col] = 1
                else:
                    corner[row, a * SHIFT_LON + col - own_cols] = 1
    return own, lat, corner


def scatter_matrices(cols_here):
    own_cols = cols_here - SHIFT_LON
    lat = place(WLAT * cols_here, SHIFT_LAT * own_cols)
    corner = place(WLAT * cols_here, WLAT * SHIFT_LON)
    for a in range(WLAT):
        for c in range(cols_here):
            row = a * cols_here + c
            if c >= SHIFT_LON:
                if a < SHIFT_LAT:
                    lat[row, a * own_cols + c - SHIFT_LON] = 1
            elif a >= SHIFT_LAT:
                corner[row, (a - SHIFT_LAT) * SHIFT_LON + c] = 1
            else:
                corner[row, (a + SHIFT_LAT) * SHIFT_LON + c] = 1
    return lat, corner


def lon_selectors():
    out = np.zeros((WLON, 3 * LANES, 2 * LANES), np.float32)
    for xj in range(WLON):
        for g in range(GROUPS):
            for xi in range(WLON):
                out[xj, g * SPAN + xi - xj + WLON - 1, g * WLON + xi] = 1
    return out


def dot(a, b, ca=1, cb=0):
    return lax.dot_general(a, b, (((ca,), (cb,)), ((), ())), preferred_element_type=F32)


def split(value):
    high = value.astype(BF)
    return high, (value - high.astype(F32)).astype(BF)


def prep_kernel(wx_ref, gx_ref, lat_pick, lon_pick, diag_pick, lat_out, lon_out, diag_out):
    def step(level, carry):
        for pick, strip in ((lat_pick, lat_out), (lon_pick, lon_out), (diag_pick, diag_out)):
            strip[level] = jnp.concatenate(
                [dot(pick[...], ref[level]) for ref in (wx_ref, gx_ref)], axis=1
            ).astype(BF)
        return carry

    lax.fori_loop(0, wx_ref.shape[0], step, 0)


def expand_kernel(lat_ref, table_ref, sel_ref, main_ref, rest_ref):
    table = table_ref[...]
    high = table.astype(BF)
    rest = table - high.astype(F32)
    mid = rest.astype(BF)
    low = (rest - mid.astype(F32)).astype(BF)
    rows = table.shape[0]
    last = lat_ref[0] == lat_ref[1]
    row_id = lax.broadcasted_iota(jnp.int32, (rows, 2 * LANES), 0)
    col_id = lax.broadcasted_iota(jnp.int32, (rows, 2 * LANES), 1)
    a_j = row_id % WLAT
    z_j = (row_id // WLAT) % WLEV
    a_i = (col_id // WLON) % WLAT
    z_i = col_id // (WLON * WLAT)
    cross_lev = jnp.logical_and(row_id >= rows * 3 // 4, z_j != z_i)
    cross_lat = jnp.logical_and(last, (a_j >= SHIFT_LAT) != (a_i >= SHIFT_LAT))
    hide = jnp.where(jnp.logical_or(cross_lev, cross_lat), MASKED, 0.0)

    def step(xj, carry):
        sel = sel_ref[xj, : GROUPS * SPAN]
        value = dot(high, sel) + dot(mid, sel) + dot(low, sel) + hide
        main_ref[pl.ds(xj, rows, stride=WLON), :] = value[:, :LANES]
        rest_ref[pl.ds(xj, rows, stride=WLON), :] = value[:, LANES:]
        return carry

    lax.fori_loop(0, WLON, step, 0)


def main_kernel(
    core_ref, wx_ref, gx_ref, lat_in, lon_in, diag_in, gain_ref, wqkv_ref, proj_ref, bias_main, bias_rest, sel_ref,
    pown_ref, plat_ref, plon_ref, pdiag_ref,
    base_ref, gbase_ref, lat_out, lon_out, diag_out, keep_ref, send_ref,
    x_s, g_s, br_s, gi_s, dsum_main, dsum_rest, gw_ref, gproj_ref, ggain_ref, gbias_ref, pay_s,
):
    channel = lax.broadcasted_iota(jnp.int32, (TOK, CH), 1)
    head_mask = [jnp.logical_and(channel >= h * HD, channel < (h + 1) * HD) for h in range(HEADS)]

    def load_level(level, carry):
        k = ((level + 7) % 8) // 2
        z = (level + 7) % 2
        place_own = pown_ref[...]
        strips = ((plat_ref, lat_in), (plon_ref, lon_in), (pdiag_ref, diag_in))
        xw = dot(place_own, wx_ref[level])
        gw = dot(place_own, gx_ref[level])
        for where_ref, strip in strips:
            both = strip[level]
            xw = xw + dot(where_ref[...], both[:, :CH])
            gw = gw + dot(where_ref[...], both[:, CH:])
        half = TOK // 2
        for n in range(2):
            x_s[2 * k + n, pl.ds(pl.multiple_of(z * half, 8), half), :] = xw[n * half : (n + 1) * half]
            g_s[2 * k + n, pl.ds(pl.multiple_of(z * half, 8), half), :] = gw[n * half : (n + 1) * half]
        return carry

    lax.fori_loop(0, 8, load_level, 0)
    dsum_main[...] = jnp.zeros_like(dsum_main)
    dsum_rest[...] = jnp.zeros_like(dsum_rest)
    gw_ref[...] = jnp.zeros_like(gw_ref)
    gproj_ref[...] = jnp.zeros_like(gproj_ref)
    ggain_ref[...] = jnp.zeros_like(ggain_ref)
    gain = gain_ref[...]
    inv_root = HD ** (-0.5)

    def eye(n):
        return (lax.broadcasted_iota(jnp.int32, (n, n), 0) == lax.broadcasted_iota(jnp.int32, (n, n), 1)).astype(F32).astype(BF)

    eye_c = eye(CH)
    eye_t = eye(TOK)

    def window(w, carry):
        k = w // 2
        x = x_s[w]
        centre = jnp.mean(x, axis=-1, keepdims=True)
        centred = x - centre
        inv_std = lax.rsqrt(jnp.mean(centred * centred, axis=-1, keepdims=True) + EPSILON)
        normed = centred * inv_std
        hidden = (normed * gain).astype(BF)
        q = (dot(hidden, wqkv_ref[0]) * inv_root).astype(BF)
        key = dot(hidden, wqkv_ref[1]).astype(BF)
        v = dot(hidden, wqkv_ref[2]).astype(BF)
        g = g_s[w].astype(BF)
        d_att = dot(g, proj_ref[...], 1, 1).astype(BF)
        key_t = dot(eye_c, key, 1, 1).astype(BF)
        v_t = dot(eye_c, v, 1, 1).astype(BF)
        zero = jnp.zeros((TOK, CH), BF)
        att_parts = []
        dq_parts = []
        d_key = jnp.zeros((TOK, CH), F32)
        d_val = jnp.zeros((TOK, CH), F32)
        for h in range(HEADS):
            lo, hi = h * HD, (h + 1) * HD
            s = dot(jnp.where(head_mask[h], key, zero), q, 1, 1)
            rows = pl.ds(pl.multiple_of((k * HEADS + h) * TOK, 8), TOK)
            s = s + jnp.concatenate([bias_main[rows, :], bias_rest[rows, : TOK - LANES]], axis=1)
            s = s - jnp.max(s, axis=0, keepdims=True)
            e = jnp.exp(s)
            probs = (e / jnp.sum(e, axis=0, keepdims=True)).astype(BF)
            dp = dot(jnp.where(head_mask[h], v, zero), d_att, 1, 1)
            att_parts.append(dot(v_t[lo:hi], probs))
            d_val = d_val + dot(probs, jnp.where(head_mask[h], d_att, zero))
            pf = probs.astype(F32)
            t = pf * dp
            ds = t - pf * jnp.sum(t, axis=0, keepdims=True)
            dsum_main[rows, :] += ds[:, :LANES]
            dsum_rest[rows, : TOK - LANES] += ds[:, LANES:]
            dsb = ds.astype(BF)
            dq_parts.append(dot(key_t[lo:hi], dsb))
            d_key = d_key + dot(dsb, jnp.where(head_mask[h], q, zero))
        att_t = jnp.concatenate(att_parts, axis=0).astype(BF)
        dq_t = (jnp.concatenate(dq_parts, axis=0) * inv_root).astype(BF)
        att = dot(eye_t, att_t, 1, 1).astype(BF)
        dq = dot(eye_t, dq_t, 1, 1).astype(BF)
        dk = d_key.astype(BF)
        dv = d_val.astype(BF)
        br_s[w] = dot(att, proj_ref[...])
        gproj_ref[...] += dot(att_t, g)
        hidden_t = dot(eye_c, hidden, 1, 1).astype(BF)
        gw_ref[0] += dot(hidden_t, dq)
        gw_ref[1] += dot(hidden_t, dk)
        gw_ref[2] += dot(hidden_t, dv)
        gh = dot(dq, wqkv_ref[0], 1, 1) + dot(dk, wqkv_ref[1], 1, 1) + dot(dv, wqkv_ref[2], 1, 1)
        ggain_ref[...] += jnp.sum(gh * normed, axis=0, keepdims=True)
        gn = gh * gain
        gi = inv_std * (
            gn
            - jnp.mean(gn, axis=-1, keepdims=True)
            - normed * jnp.mean(gn * normed, axis=-1, keepdims=True)
        )
        gi_s[w] = gi
        return carry

    lax.fori_loop(0, 8, window, 0)

    def store_level(level, carry):
        k = ((level + 7) % 8) // 2
        z = (level + 7) % 2
        half = TOK // 2
        moved = []
        for src, own_in, own_out in ((br_s, wx_ref, base_ref), (gi_s, gx_ref, gbase_ref)):
            rows = jnp.concatenate(
                [src[2 * k + n, pl.ds(pl.multiple_of(z * half, 8), half), :] for n in range(2)], axis=0
            ).astype(BF)
            own_out[level] = (own_in[level].astype(F32) + dot(pown_ref[...], rows, 0, 0)).astype(BF)
            moved.append(rows)
        for where_ref, strip in ((plat_ref, lat_out), (plon_ref, lon_out), (pdiag_ref, diag_out)):
            strip[level] = jnp.concatenate(
                [dot(where_ref[...], rows, 0, 0) for rows in moved], axis=1
            ).astype(BF)
        return carry

    lax.fori_loop(0, 8, store_level, 0)

    gbias_ref[...] = jnp.zeros_like(gbias_ref)
    pairs = dsum_main.shape[0] // TOK

    def fold_step(xj, carry):
        blocks = []
        for m in range(GROUPS):
            rows = pl.ds(m * WLON + xj, pairs, stride=TOK)
            blocks.append(jnp.concatenate([dsum_main[rows, :], dsum_rest[rows, :]], axis=1))
        high, low = split(jnp.concatenate(blocks, axis=0))
        sel = sel_ref[xj]
        gbias_ref[...] += dot(high, sel, 1, 1) + dot(low, sel, 1, 1)
        return carry

    lax.fori_loop(0, WLON, fold_step, 0)
    weights = jnp.concatenate([gw_ref[0], gw_ref[1], gw_ref[2], gproj_ref[...]], axis=1)
    for j in range(WTILES):
        pay_s[j * CH : (j + 1) * CH, :] = weights[:, j * LANES : (j + 1) * LANES]
    for j in range(3):
        pay_s[BROW + j * BIAS_ROWS : BROW + (j + 1) * BIAS_ROWS, :] = gbias_ref[:, j * LANES : (j + 1) * LANES]
    pay_s[GROW:, :] = jnp.zeros((PAY - GROW, LANES), F32)
    pay_s[GROW : GROW + 1, :] = ggain_ref[:, :LANES]
    pay_s[GROW + 1 : GROW + 2, : CH - LANES] = ggain_ref[:, LANES:]
    core = core_ref[0]
    half_rows = PAY // 2
    keep_ref[...] = pay_s[pl.ds(pl.multiple_of(core * half_rows, half_rows), half_rows), :].astype(BF)
    send_ref[...] = pay_s[pl.ds(pl.multiple_of((1 - core) * half_rows, half_rows), half_rows), :].astype(BF)


def finish_kernel(
    factor, core_ref, base_ref, gbase_ref, lat_in, lon_in, diag_in, slat_ref, slon_ref, sdiag_ref, mine_ref, other_ref,
    out_ref, gout_ref, gqkv_ref, gproj_ref, ggain_ref, gbias_ref, full_s, table_s,
):
    core = core_ref[0]
    half_rows = PAY // 2
    full_s[pl.ds(pl.multiple_of(core * half_rows, half_rows), half_rows), :] = mine_ref[...].astype(F32) * factor
    full_s[pl.ds(pl.multiple_of((1 - core) * half_rows, half_rows), half_rows), :] = other_ref[...].astype(F32) * factor
    tiles = [full_s[j * CH : (j + 1) * CH, :] for j in range(WTILES)]
    for j in range(4):
        gqkv_ref[:, j * LANES : (j + 1) * LANES] = tiles[j]
    cut = 3 * CH - 4 * LANES
    gqkv_ref[:, 4 * LANES :] = tiles[4][:, :cut]
    gproj_ref[...] = jnp.concatenate([tiles[4][:, cut:], tiles[5]], axis=1)
    ggain_ref[...] = jnp.concatenate(
        [full_s[GROW : GROW + 1, :], full_s[GROW + 1 : GROW + 2, : CH - LANES]], axis=1
    )
    pairs = BIAS_ROWS // GROUPS
    for m in range(GROUPS):
        z_j, a_j = divmod(m, WLAT)
        block = jnp.concatenate(
            [full_s[BROW + j * BIAS_ROWS + m * pairs : BROW + j * BIAS_ROWS + (m + 1) * pairs, :] for j in range(3)],
            axis=1,
        )
        for g in range(GROUPS):
            z_i, a_i = divmod(g, WLAT)
            to = SPAN * (((z_i * WLEV + z_j) * WLAT + a_i) * WLAT + a_j)
            table_s[:, to : to + SPAN] = block[:, g * SPAN : (g + 1) * SPAN]
    for r in range(pairs):
        gbias_ref[r] = table_s[r : r + 1, : gbias_ref.shape[2]]

    def step(level, carry):
        up = base_ref[level].astype(F32)
        gup = gbase_ref[level].astype(F32)
        for where_ref, strip in ((slat_ref, lat_in), (slon_ref, lon_in), (sdiag_ref, diag_in)):
            both = strip[level]
            up = up + dot(where_ref[...], both[:, :CH])
            gup = gup + dot(where_ref[...], both[:, CH:])
        out_ref[level] = up.astype(BF)
        gout_ref[level] = gup.astype(BF)
        return carry

    lax.fori_loop(0, 8, step, 0)


def passed(value, lat_step, lon_step):
    lats, highs, zs = lax.axis_size("lat"), lax.axis_size("yhi"), lax.axis_size("z")
    lons = highs * zs
    pairs = [
        (b * lats + a, (b + lon_step) % lons * lats + (a + lat_step) % lats)
        for b in range(lons)
        for a in range(lats)
    ]
    return lax.ppermute(value, ("yhi", "z", "lat"), pairs)


def swapped(value):
    return lax.ppermute(value, "core", [(0, 1), (1, 0)])


def total_over_devices(keep, send):
    wide = ("ylo", "yhi", "z")
    peers = lax.axis_size("ylo") * lax.axis_size("yhi") * lax.axis_size("z")
    half = (keep.astype(F32) + swapped(send).astype(F32)).astype(BF)
    pieces = lax.all_to_all(half, wide, 0, 0, tiled=True)
    piece = jnp.sum(pieces.reshape(peers, PIECE, LANES).astype(F32), axis=0)
    lats = lax.axis_size("lat")
    place_here = lax.axis_index("core") * peers + lax.axis_index(wide)
    shared = jnp.logical_or(place_here < BROW // PIECE, place_here >= GROW // PIECE)
    others = jnp.zeros_like(piece)
    for step in range(1, lats):
        others = others + lax.ppermute(piece, "lat", [(a, (a + step) % lats) for a in range(lats)])
    piece = jnp.where(shared, piece + others, piece).astype(BF)
    spread = jnp.broadcast_to(piece[None], (peers, PIECE, LANES)).reshape(half.shape)
    mine = lax.all_to_all(spread, wide, 0, 0, tiled=True)
    return mine, swapped(mine)


def call(kernel, out_shape, scratch=(), smem=0, count=0, flops=0):
    specs = [pl.BlockSpec(memory_space=pltpu.SMEM)] * smem
    specs += [pl.BlockSpec(memory_space=pltpu.VMEM)] * (count - smem)
    return pl.pallas_call(
        kernel,
        out_shape=out_shape,
        in_specs=specs,
        out_specs=jax.tree.map(lambda _: pl.BlockSpec(memory_space=pltpu.VMEM), out_shape),
        scratch_shapes=list(scratch),
        compiler_params=pltpu.CompilerParams(vmem_limit_bytes=VMEM_LIMIT),
        cost_estimate=pl.CostEstimate(flops=flops, bytes_accessed=flops // 500, transcendentals=0),
    )


def sds(shape, dtype):
    return jax.ShapeDtypeStruct(shape, dtype)


def shards(weather, cotangent, norm_gain, qkv_weight, proj_weight, bias_table):
    samples, levels, rows_here, cols_here, channels = weather.shape
    lat_index = lax.axis_index("lat")
    lat_count = lax.axis_size("lat")
    plane = rows_here * cols_here
    own_cols = cols_here - SHIFT_LON
    wx = weather.reshape(levels, plane, CH)
    gx = cotangent.reshape(levels, plane, CH)
    edge = SHIFT_LAT * SHIFT_LON
    lat_shape = sds((levels, SHIFT_LAT * own_cols, 2 * CH), BF)
    edge_shape = sds((levels, edge, 2 * CH), BF)
    slat, scor = scatter_matrices(cols_here)
    scatter = (slat, scor[:, :edge], scor[:, edge:])
    strips = call(prep_kernel, (lat_shape, edge_shape, edge_shape), count=5, flops=10**9)(
        wx, gx, *[jnp.asarray(m.T, BF) for m in scatter]
    )
    lat_in = passed(strips[0], -1, 0)
    lon_in = passed(strips[1], 0, -1)
    diag_in = passed(strips[2], -1, -1)

    lev_windows = bias_table.shape[0]
    table = bias_table.reshape(lev_windows, HEADS, WLEV, WLEV, WLAT, WLAT, SPAN)
    table = table.transpose(0, 1, 3, 5, 2, 4, 6).reshape(lev_windows * HEADS * GROUPS, GROUPS * SPAN)
    place_lat = jnp.stack([lat_index, lat_count - 1]).astype(jnp.int32)
    sel = jnp.asarray(lon_selectors(), BF)
    bias_rows = lev_windows * HEADS * TOK
    bias_shape = sds((bias_rows, LANES), F32)
    bias_main, bias_rest = call(
        expand_kernel, (bias_shape, bias_shape), smem=1, count=3, flops=10**9
    )(place_lat, table, sel)

    own_m, lat_m, corner_m = gather_matrices(cols_here)
    mats = [jnp.asarray(m, BF) for m in (own_m, lat_m, corner_m[:, :edge], corner_m[:, edge:])]
    wqkv = qkv_weight.reshape(CH, 3, CH).transpose(1, 0, 2)
    n_win = 8
    plane_shape = sds((levels, plane, CH), BF)
    core = lax.axis_index("core").astype(jnp.int32).reshape(1)
    half_shape = sds((PAY // 2, LANES), BF)
    base, gbase, lat_out, lon_out, diag_out, keep, send = call(
        main_kernel,
        (
            plane_shape, plane_shape, lat_shape, edge_shape, edge_shape,
            half_shape, half_shape,
        ),
        scratch=[pltpu.VMEM((n_win, TOK, CH), F32)] * 4
        + [pltpu.VMEM((bias_rows, LANES), F32)] * 2
        + [
            pltpu.VMEM((3, CH, CH), F32), pltpu.VMEM((CH, CH), F32), pltpu.VMEM((1, CH), F32),
            pltpu.VMEM((BIAS_ROWS, 3 * LANES), F32), pltpu.VMEM((PAY, LANES), F32),
        ],
        smem=1,
        count=16,
        flops=10**10,
    )(core, wx, gx, lat_in, lon_in, diag_in, norm_gain.reshape(1, CH), wqkv, proj_weight, bias_main, bias_rest, sel, *mats)

    lat_back = passed(lat_out, 1, 0)
    lon_back = passed(lon_out, 0, 1)
    diag_back = passed(diag_out, 1, 1)
    mine, other = total_over_devices(keep, send)
    factor = (samples * levels * rows_here * cols_here * lax.axis_size(("ylo", "core", "yhi", "z", "lat"))) ** (-0.5)
    pairs = lev_windows * HEADS
    entries = bias_table.shape[-1]
    out, gout, gqkv, gproj, ggain, gbias = call(
        functools.partial(finish_kernel, factor),
        (
            plane_shape, plane_shape, sds(qkv_weight.shape, F32), sds(proj_weight.shape, F32),
            sds((1, CH), F32), sds((pairs, 1, entries), F32),
        ),
        scratch=[pltpu.VMEM((PAY, LANES), F32), pltpu.VMEM((pairs, -(-entries // LANES) * LANES), F32)],
        smem=1,
        count=11,
        flops=10**9,
    )(core, base, gbase, lat_back, lon_back, diag_back, *[jnp.asarray(m, BF) for m in scatter], mine, other)
    return (
        out.reshape(weather.shape),
        gout.reshape(weather.shape),
        gqkv,
        gproj,
        ggain.reshape(CH),
        gbias.reshape(lev_windows, HEADS, 1, entries).transpose(0, 2, 1, 3),
    )


def solution(mesh):
    fine = jax.sharding.Mesh(mesh.devices.reshape(2, 2, 2, 8, 4), ("ylo", "core", "yhi", "z", "lat"))
    dp, lon = ("ylo", "core"), ("yhi", "z")
    grid = P(dp, None, "lat", lon, None)
    table = P(None, "lat", None, None)
    return jax.shard_map(
        shards,
        mesh=fine,
        in_specs=(grid, grid, P(), P(), P(), table),
        out_specs=(grid, grid, P(), P(), P(), table),
        check_vma=False,
    )
```

```python
import functools

import numpy as np
import jax
import jax.numpy as jnp
from jax import lax
from jax.experimental import pallas as pl
from jax.experimental.pallas import tpu as pltpu
from jax.sharding import PartitionSpec as P

HEADS = 6
WLEV = 2
WLAT = 6
WLON = 12
HD = 32
CH = 192
TOK = 144
LANES = 128
SHIFT_LAT = 3
SHIFT_LON = 6
SPAN = 2 * WLON - 1
GROUPS = WLEV * WLAT
MASKED = -1e30
EPSILON = 1e-05
BF = jnp.bfloat16
F32 = jnp.float32
PAY = 2048
WTILES = 6
BIAS_ROWS = 288
BROW = WTILES * CH
GROW = BROW + 3 * BIAS_ROWS
PIECE = 32
VMEM_LIMIT = 56 * 1024 * 1024


def place(rows, cols):
    return np.zeros((rows, cols), np.float32)


def gather_matrices(cols_here):
    windows = cols_here // WLON
    own_cols = cols_here - SHIFT_LON
    own = place(windows * WLAT * WLON, WLAT * cols_here)
    lat = place(windows * WLAT * WLON, SHIFT_LAT * own_cols)
    corner = place(windows * WLAT * WLON, WLAT * SHIFT_LON)
    for n in range(windows):
        for a in range(WLAT):
            for x in range(WLON):
                row = (n * WLAT + a) * WLON + x
                col = n * WLON + x
                if col < own_cols:
                    if a < SHIFT_LAT:
                        own[row, (a + SHIFT_LAT) * cols_here + col + SHIFT_LON] = 1
                    else:
                        lat[row, (a - SHIFT_LAT) * own_cols + col] = 1
                else:
                    corner[row, a * SHIFT_LON + col - own_cols] = 1
    return own, lat, corner


def scatter_matrices(cols_here):
    own_cols = cols_here - SHIFT_LON
    lat = place(WLAT * cols_here, SHIFT_LAT * own_cols)
    corner = place(WLAT * cols_here, WLAT * SHIFT_LON)
    for a in range(WLAT):
        for c in range(cols_here):
            row = a * cols_here + c
            if c >= SHIFT_LON:
                if a < SHIFT_LAT:
                    lat[row, a * own_cols + c - SHIFT_LON] = 1
            elif a >= SHIFT_LAT:
                corner[row, (a - SHIFT_LAT) * SHIFT_LON + c] = 1
            else:
                corner[row, (a + SHIFT_LAT) * SHIFT_LON + c] = 1
    return lat, corner


def lon_selectors():
    out = np.zeros((WLON, 3 * LANES, 2 * LANES), np.float32)
    for xj in range(WLON):
        for g in range(GROUPS):
            for xi in range(WLON):
                out[xj, g * SPAN + xi - xj + WLON - 1, g * WLON + xi] = 1
    return out


def dot(a, b, ca=1, cb=0):
    return lax.dot_general(a, b, (((ca,), (cb,)), ((), ())), preferred_element_type=F32)


def split(value):
    high = value.astype(BF)
    return high, (value - high.astype(F32)).astype(BF)


def prep_kernel(wx_ref, gx_ref, lat_pick, lon_pick, diag_pick, lat_out, lon_out, diag_out):
    def step(level, carry):
        for pick, strip in ((lat_pick, lat_out), (lon_pick, lon_out), (diag_pick, diag_out)):
            strip[level] = jnp.concatenate(
                [dot(pick[...], ref[level]) for ref in (wx_ref, gx_ref)], axis=1
            ).astype(BF)
        return carry

    lax.fori_loop(0, wx_ref.shape[0], step, 0, unroll=True)


def expand_kernel(last_ref, table_ref, sel_ref, main_ref, rest_ref, flat_s, table_s):
    pairs, _, entries = table_ref.shape
    for r in range(pairs):
        flat_s[r : r + 1, :entries] = table_ref[r]
    for m in range(GROUPS):
        z_j, a_j = divmod(m, WLAT)
        for g in range(GROUPS):
            z_i, a_i = divmod(g, WLAT)
            at = SPAN * (((z_i * WLEV + z_j) * WLAT + a_i) * WLAT + a_j)
            table_s[m * pairs : (m + 1) * pairs, g * SPAN : (g + 1) * SPAN] = flat_s[:, at : at + SPAN]
    high, low = split(table_s[...])
    rows = BIAS_ROWS
    row_id = lax.broadcasted_iota(jnp.int32, (rows, 2 * LANES), 0)
    col_id = lax.broadcasted_iota(jnp.int32, (rows, 2 * LANES), 1)
    z_j = row_id // (WLAT * pairs)
    a_j = row_id // pairs % WLAT
    lev = row_id % pairs // HEADS
    a_i = col_id // WLON % WLAT
    z_i = col_id // (WLON * WLAT)
    cross_lev = jnp.logical_and(lev == pairs // HEADS - 1, z_j != z_i)
    cross_lat = jnp.logical_and(last_ref[0] == 1, (a_j >= SHIFT_LAT) != (a_i >= SHIFT_LAT))
    hide = jnp.where(jnp.logical_or(cross_lev, cross_lat), MASKED, 0.0)

    def step(xj, carry):
        sel = sel_ref[xj, : GROUPS * SPAN]
        value = dot(high, sel) + dot(low, sel) + hide
        for m in range(GROUPS):
            at = pl.ds(m * WLON + xj, pairs, stride=TOK)
            main_ref[at, :] = value[m * pairs : (m + 1) * pairs, :LANES]
            rest_ref[at, :] = value[m * pairs : (m + 1) * pairs, LANES:]
        return carry

    lax.fori_loop(0, WLON, step, 0, unroll=4)


def main_kernel(
    core_ref, wx_ref, gx_ref, lat_in, lon_in, diag_in, gain_ref, wqkv_ref, proj_ref, bias_main, bias_rest, sel_ref,
    pown_ref, plat_ref, plon_ref, pdiag_ref,
    base_ref, gbase_ref, lat_out, lon_out, diag_out, keep_ref, send_ref,
    x_s, g_s, br_s, gi_s, dsum_main, dsum_rest, gw_ref, gproj_ref, ggain_ref, gbias_ref, pay_s,
):
    channel = lax.broadcasted_iota(jnp.int32, (TOK, CH), 1)
    head_mask = [jnp.logical_and(channel >= h * HD, channel < (h + 1) * HD) for h in range(HEADS)]

    def load_level(level, carry):
        k = ((level + 7) % 8) // 2
        z = (level + 7) % 2
        place_own = pown_ref[...]
        strips = ((plat_ref, lat_in), (plon_ref, lon_in), (pdiag_ref, diag_in))
        xw = dot(place_own, wx_ref[level])
        gw = dot(place_own, gx_ref[level])
        for where_ref, strip in strips:
            both = strip[level]
            xw = xw + dot(where_ref[...], both[:, :CH])
            gw = gw + dot(where_ref[...], both[:, CH:])
        half = TOK // 2
        for n in range(2):
            x_s[2 * k + n, pl.ds(pl.multiple_of(z * half, 8), half), :] = xw[n * half : (n + 1) * half]
            g_s[2 * k + n, pl.ds(pl.multiple_of(z * half, 8), half), :] = gw[n * half : (n + 1) * half]
        return carry

    lax.fori_loop(0, 8, load_level, 0, unroll=True)
    dsum_main[...] = jnp.zeros_like(dsum_main)
    dsum_rest[...] = jnp.zeros_like(dsum_rest)
    gw_ref[...] = jnp.zeros_like(gw_ref)
    gproj_ref[...] = jnp.zeros_like(gproj_ref)
    ggain_ref[...] = jnp.zeros_like(ggain_ref)
    gain = gain_ref[...]
    inv_root = HD ** (-0.5)

    def eye(n):
        return (lax.broadcasted_iota(jnp.int32, (n, n), 0) == lax.broadcasted_iota(jnp.int32, (n, n), 1)).astype(F32).astype(BF)

    eye_c = eye(CH)
    eye_t = eye(TOK)

    def window(w, carry):
        k = w // 2
        x = x_s[w]
        centre = jnp.mean(x, axis=-1, keepdims=True)
        centred = x - centre
        inv_std = lax.rsqrt(jnp.mean(centred * centred, axis=-1, keepdims=True) + EPSILON)
        normed = centred * inv_std
        hidden = (normed * gain).astype(BF)
        q = (dot(hidden, wqkv_ref[0]) * inv_root).astype(BF)
        key = dot(hidden, wqkv_ref[1]).astype(BF)
        v = dot(hidden, wqkv_ref[2]).astype(BF)
        g = g_s[w].astype(BF)
        d_att = dot(g, proj_ref[...], 1, 1).astype(BF)
        key_t = dot(eye_c, key, 1, 1).astype(BF)
        v_t = dot(eye_c, v, 1, 1).astype(BF)
        zero = jnp.zeros((TOK, CH), BF)

        def per_head(value):
            return jnp.concatenate([jnp.where(mask, value, zero) for mask in head_mask], axis=0)

        def own_head(value):
            total = jnp.where(head_mask[0], value[:TOK], 0.0)
            for h in range(1, HEADS):
                total = jnp.where(head_mask[h], value[h * TOK : (h + 1) * TOK], total)
            return total

        rows = pl.ds(pl.multiple_of(k * HEADS * TOK, 8), HEADS * TOK)
        scores = dot(per_head(key), q, 1, 1)
        scores = scores + jnp.concatenate([bias_main[rows, :], bias_rest[rows, : TOK - LANES]], axis=1)
        scores = scores.reshape(HEADS, TOK, TOK)
        dp = dot(per_head(v), d_att, 1, 1).reshape(HEADS, TOK, TOK)
        e = jnp.exp(scores - jnp.max(scores, axis=1, keepdims=True))
        probs = (e * (1.0 / jnp.sum(e, axis=1, keepdims=True))).astype(BF)
        d_val = own_head(dot(probs.reshape(HEADS * TOK, TOK), d_att))
        pf = probs.astype(F32)
        t = pf * dp
        ds = t - pf * jnp.sum(t, axis=1, keepdims=True)
        dsb = ds.astype(BF)
        ds = ds.reshape(HEADS * TOK, TOK)
        dsum_main[rows, :] += ds[:, :LANES]
        dsum_rest[rows, : TOK - LANES] += ds[:, LANES:]
        d_key = own_head(dot(dsb.reshape(HEADS * TOK, TOK), q))
        att_parts = [dot(v_t[h * HD : (h + 1) * HD], probs[h]) for h in range(HEADS)]
        dq_parts = [dot(key_t[h * HD : (h + 1) * HD], dsb[h]) for h in range(HEADS)]
        att_t = jnp.concatenate(att_parts, axis=0).astype(BF)
        dq_t = (jnp.concatenate(dq_parts, axis=0) * inv_root).astype(BF)
        att = dot(eye_t, att_t, 1, 1).astype(BF)
        dq = dot(eye_t, dq_t, 1, 1).astype(BF)
        dk = d_key.astype(BF)
        dv = d_val.astype(BF)
        br_s[w] = dot(att, proj_ref[...])
        gproj_ref[...] += dot(att_t, g)
        hidden_t = dot(eye_c, hidden, 1, 1).astype(BF)
        gw_ref[0] += dot(hidden_t, dq)
        gw_ref[1] += dot(hidden_t, dk)
        gw_ref[2] += dot(hidden_t, dv)
        gh = dot(dq, wqkv_ref[0], 1, 1) + dot(dk, wqkv_ref[1], 1, 1) + dot(dv, wqkv_ref[2], 1, 1)
        ggain_ref[...] += jnp.sum(gh * normed, axis=0, keepdims=True)
        gn = gh * gain
        gi = inv_std * (
            gn
            - jnp.mean(gn, axis=-1, keepdims=True)
            - normed * jnp.mean(gn * normed, axis=-1, keepdims=True)
        )
        gi_s[w] = gi
        return carry

    lax.fori_loop(0, 8, window, 0)

    def store_level(level, carry):
        k = ((level + 7) % 8) // 2
        z = (level + 7) % 2
        half = TOK // 2
        moved = []
        for src, own_in, own_out in ((br_s, wx_ref, base_ref), (gi_s, gx_ref, gbase_ref)):
            rows = jnp.concatenate(
                [src[2 * k + n, pl.ds(pl.multiple_of(z * half, 8), half), :] for n in range(2)], axis=0
            ).astype(BF)
            own_out[level] = (own_in[level].astype(F32) + dot(pown_ref[...], rows, 0, 0)).astype(BF)
            moved.append(rows)
        for where_ref, strip in ((plat_ref, lat_out), (plon_ref, lon_out), (pdiag_ref, diag_out)):
            strip[level] = jnp.concatenate(
                [dot(where_ref[...], rows, 0, 0) for rows in moved], axis=1
            ).astype(BF)
        return carry

    lax.fori_loop(0, 8, store_level, 0, unroll=True)

    gbias_ref[...] = jnp.zeros_like(gbias_ref)
    pairs = dsum_main.shape[0] // TOK

    def fold_step(xj, carry):
        blocks = []
        for m in range(GROUPS):
            rows = pl.ds(m * WLON + xj, pairs, stride=TOK)
            blocks.append(jnp.concatenate([dsum_main[rows, :], dsum_rest[rows, :]], axis=1))
        high, low = split(jnp.concatenate(blocks, axis=0))
        sel = sel_ref[xj]
        gbias_ref[...] += dot(high, sel, 1, 1) + dot(low, sel, 1, 1)
        return carry

    lax.fori_loop(0, WLON, fold_step, 0)
    weights = jnp.concatenate([gw_ref[0], gw_ref[1], gw_ref[2], gproj_ref[...]], axis=1)
    for j in range(WTILES):
        pay_s[j * CH : (j + 1) * CH, :] = weights[:, j * LANES : (j + 1) * LANES]
    for j in range(3):
        pay_s[BROW + j * BIAS_ROWS : BROW + (j + 1) * BIAS_ROWS, :] = gbias_ref[:, j * LANES : (j + 1) * LANES]
    pay_s[GROW:, :] = jnp.zeros((PAY - GROW, LANES), F32)
    pay_s[GROW : GROW + 1, :] = ggain_ref[:, :LANES]
    pay_s[GROW + 1 : GROW + 2, : CH - LANES] = ggain_ref[:, LANES:]
    core = core_ref[0]
    half_rows = PAY // 2
    keep_ref[...] = pay_s[pl.ds(pl.multiple_of(core * half_rows, half_rows), half_rows), :].astype(BF)
    send_ref[...] = pay_s[pl.ds(pl.multiple_of((1 - core) * half_rows, half_rows), half_rows), :].astype(BF)


def finish_kernel(
    factor, core_ref, base_ref, gbase_ref, lat_in, lon_in, diag_in, slat_ref, slon_ref, sdiag_ref, mine_ref, other_ref,
    out_ref, gout_ref, gqkv_ref, gproj_ref, ggain_ref, gbias_ref, full_s, table_s,
):
    core = core_ref[0]
    half_rows = PAY // 2
    full_s[pl.ds(pl.multiple_of(core * half_rows, half_rows), half_rows), :] = mine_ref[...].astype(F32) * factor
    full_s[pl.ds(pl.multiple_of((1 - core) * half_rows, half_rows), half_rows), :] = other_ref[...].astype(F32) * factor
    tiles = [full_s[j * CH : (j + 1) * CH, :] for j in range(WTILES)]
    for j in range(4):
        gqkv_ref[:, j * LANES : (j + 1) * LANES] = tiles[j]
    cut = 3 * CH - 4 * LANES
    gqkv_ref[:, 4 * LANES :] = tiles[4][:, :cut]
    gproj_ref[...] = jnp.concatenate([tiles[4][:, cut:], tiles[5]], axis=1)
    ggain_ref[...] = jnp.concatenate(
        [full_s[GROW : GROW + 1, :], full_s[GROW + 1 : GROW + 2, : CH - LANES]], axis=1
    )
    pairs = BIAS_ROWS // GROUPS
    for m in range(GROUPS):
        z_j, a_j = divmod(m, WLAT)
        block = jnp.concatenate(
            [full_s[BROW + j * BIAS_ROWS + m * pairs : BROW + j * BIAS_ROWS + (m + 1) * pairs, :] for j in range(3)],
            axis=1,
        )
        for g in range(GROUPS):
            z_i, a_i = divmod(g, WLAT)
            to = SPAN * (((z_i * WLEV + z_j) * WLAT + a_i) * WLAT + a_j)
            table_s[:, to : to + SPAN] = block[:, g * SPAN : (g + 1) * SPAN]
    for r in range(pairs):
        gbias_ref[r] = table_s[r : r + 1, : gbias_ref.shape[2]]

    def step(level, carry):
        up = base_ref[level].astype(F32)
        gup = gbase_ref[level].astype(F32)
        for where_ref, strip in ((slat_ref, lat_in), (slon_ref, lon_in), (sdiag_ref, diag_in)):
            both = strip[level]
            up = up + dot(where_ref[...], both[:, :CH])
            gup = gup + dot(where_ref[...], both[:, CH:])
        out_ref[level] = up.astype(BF)
        gout_ref[level] = gup.astype(BF)
        return carry

    lax.fori_loop(0, 8, step, 0, unroll=True)


def passed(value, lat_step, lon_step):
    lats, highs, zs = lax.axis_size("lat"), lax.axis_size("yhi"), lax.axis_size("z")
    lons = highs * zs
    pairs = [
        (b * lats + a, (b + lon_step) % lons * lats + (a + lat_step) % lats)
        for b in range(lons)
        for a in range(lats)
    ]
    return lax.ppermute(value, ("yhi", "z", "lat"), pairs)


def swapped(value):
    return lax.ppermute(value, "core", [(0, 1), (1, 0)])


def total_over_devices(keep, send, backs):
    wide = ("ylo", "yhi", "z")
    peers = lax.axis_size("ylo") * lax.axis_size("yhi") * lax.axis_size("z")
    half = (keep.astype(F32) + swapped(send).astype(F32)).astype(BF)
    pieces = lax.all_to_all(half, wide, 0, 0, tiled=True)
    piece = jnp.sum(pieces.reshape(peers, PIECE, LANES).astype(F32), axis=0)
    lats = lax.axis_size("lat")
    place_here = lax.axis_index("core") * peers + lax.axis_index(wide)
    shared = jnp.logical_or(place_here < BROW // PIECE, place_here >= GROW // PIECE)
    others = jnp.zeros_like(piece)
    for step in range(1, lats):
        others = others + lax.ppermute(piece, "lat", [(a, (a + step) % lats) for a in range(lats)])
    piece = jnp.where(shared, piece + others, piece).astype(BF)
    spread = jnp.broadcast_to(piece[None], (peers, PIECE, LANES)).reshape(half.shape)
    spread, backs = lax.optimization_barrier((spread, backs))
    mine = lax.all_to_all(spread, wide, 0, 0, tiled=True)
    return mine, swapped(mine), backs


def call(kernel, out_shape, scratch=(), smem=0, count=0, flops=0):
    specs = [pl.BlockSpec(memory_space=pltpu.SMEM)] * smem
    specs += [pl.BlockSpec(memory_space=pltpu.VMEM)] * (count - smem)
    return pl.pallas_call(
        kernel,
        out_shape=out_shape,
        in_specs=specs,
        out_specs=jax.tree.map(lambda _: pl.BlockSpec(memory_space=pltpu.VMEM), out_shape),
        scratch_shapes=list(scratch),
        compiler_params=pltpu.CompilerParams(vmem_limit_bytes=VMEM_LIMIT),
        cost_estimate=pl.CostEstimate(flops=flops, bytes_accessed=flops // 500, transcendentals=0),
    )


def sds(shape, dtype):
    return jax.ShapeDtypeStruct(shape, dtype)


def shards(weather, cotangent, norm_gain, qkv_weight, proj_weight, bias_table):
    samples, levels, rows_here, cols_here, channels = weather.shape
    lat_index = lax.axis_index("lat")
    lat_count = lax.axis_size("lat")
    plane = rows_here * cols_here
    own_cols = cols_here - SHIFT_LON
    wx = weather.reshape(levels, plane, CH)
    gx = cotangent.reshape(levels, plane, CH)
    edge = SHIFT_LAT * SHIFT_LON
    lat_shape = sds((levels, SHIFT_LAT * own_cols, 2 * CH), BF)
    edge_shape = sds((levels, edge, 2 * CH), BF)
    slat, scor = scatter_matrices(cols_here)
    scatter = (slat, scor[:, :edge], scor[:, edge:])
    strips = call(prep_kernel, (lat_shape, edge_shape, edge_shape), count=5, flops=10**9)(
        wx, gx, *[jnp.asarray(m.T, BF) for m in scatter]
    )
    lat_in = passed(strips[0], -1, 0)
    lon_in = passed(strips[1], 0, -1)
    diag_in = passed(strips[2], -1, -1)

    lev_windows = bias_table.shape[0]
    pairs = lev_windows * HEADS
    entries = bias_table.shape[-1]
    table = bias_table.transpose(0, 2, 1, 3).reshape(pairs, 1, entries)
    last = (lat_index == lat_count - 1).astype(jnp.int32).reshape(1)
    sel = jnp.asarray(lon_selectors(), BF)
    bias_rows = pairs * TOK
    bias_shape = sds((bias_rows, LANES), F32)
    flat_shape = pltpu.VMEM((pairs, -(-entries // LANES) * LANES), F32)
    bias_main, bias_rest = call(
        expand_kernel, (bias_shape, bias_shape), scratch=[flat_shape, pltpu.VMEM((BIAS_ROWS, GROUPS * SPAN), F32)],
        smem=1, count=3, flops=10**9,
    )(last, table, sel)

    own_m, lat_m, corner_m = gather_matrices(cols_here)
    mats = [jnp.asarray(m, BF) for m in (own_m, lat_m, corner_m[:, :edge], corner_m[:, edge:])]
    wqkv = qkv_weight.reshape(CH, 3, CH).transpose(1, 0, 2)
    n_win = 8
    plane_shape = sds((levels, plane, CH), BF)
    core = lax.axis_index("core").astype(jnp.int32).reshape(1)
    half_shape = sds((PAY // 2, LANES), BF)
    base, gbase, lat_out, lon_out, diag_out, keep, send = call(
        main_kernel,
        (
            plane_shape, plane_shape, lat_shape, edge_shape, edge_shape,
            half_shape, half_shape,
        ),
        scratch=[pltpu.VMEM((n_win, TOK, CH), F32)] * 4
        + [pltpu.VMEM((bias_rows, LANES), F32)] * 2
        + [
            pltpu.VMEM((3, CH, CH), F32), pltpu.VMEM((CH, CH), F32), pltpu.VMEM((1, CH), F32),
            pltpu.VMEM((BIAS_ROWS, 3 * LANES), F32), pltpu.VMEM((PAY, LANES), F32),
        ],
        smem=1,
        count=16,
        flops=10**10,
    )(core, wx, gx, lat_in, lon_in, diag_in, norm_gain.reshape(1, CH), wqkv, proj_weight, bias_main, bias_rest, sel, *mats)

    lat_back = passed(lat_out, 1, 0)
    lon_back = passed(lon_out, 0, 1)
    diag_back = passed(diag_out, 1, 1)
    mine, other, backs = total_over_devices(keep, send, (lat_back, lon_back, diag_back))
    factor = (samples * levels * rows_here * cols_here * lax.axis_size(("ylo", "core", "yhi", "z", "lat"))) ** (-0.5)
    out, gout, gqkv, gproj, ggain, gbias = call(
        functools.partial(finish_kernel, factor),
        (
            plane_shape, plane_shape, sds(qkv_weight.shape, F32), sds(proj_weight.shape, F32),
            sds((1, CH), F32), sds((pairs, 1, entries), F32),
        ),
        scratch=[pltpu.VMEM((PAY, LANES), F32), flat_shape],
        smem=1,
        count=11,
        flops=10**9,
    )(core, base, gbase, *backs, *[jnp.asarray(m, BF) for m in scatter], mine, other)
    return (
        out.reshape(weather.shape),
        gout.reshape(weather.shape),
        gqkv,
        gproj,
        ggain.reshape(CH),
        gbias.reshape(lev_windows, HEADS, 1, entries).transpose(0, 2, 1, 3),
    )


def solution(mesh):
    fine = jax.sharding.Mesh(mesh.devices.reshape(2, 2, 2, 8, 4), ("ylo", "core", "yhi", "z", "lat"))
    dp, lon = ("ylo", "core"), ("yhi", "z")
    grid = P(dp, None, "lat", lon, None)
    table = P(None, "lat", None, None)
    return jax.shard_map(
        shards,
        mesh=fine,
        in_specs=(grid, grid, P(), P(), P(), table),
        out_specs=(grid, grid, P(), P(), P(), table),
        check_vma=False,
    )
```

```python
import functools

import numpy as np
import jax
import jax.numpy as jnp
from jax import lax
from jax.experimental import pallas as pl
from jax.experimental.pallas import tpu as pltpu
from jax.sharding import PartitionSpec as P

HEADS = 6
WLEV = 2
WLAT = 6
WLON = 12
HD = 32
CH = 192
TOK = 144
LANES = 128
SHIFT_LAT = 3
SHIFT_LON = 6
SPAN = 2 * WLON - 1
GROUPS = WLEV * WLAT
MASKED = -1e30
EPSILON = 1e-05
BF = jnp.bfloat16
F32 = jnp.float32
PAY = 2048
WTILES = 6
BIAS_ROWS = 288
BROW = WTILES * CH
GROW = BROW + 3 * BIAS_ROWS
PIECE = 32
HTILES = 7
HLANES = HTILES * LANES
CHUNK = 3 * LANES
VMEM_LIMIT = 56 * 1024 * 1024


def place(rows, cols):
    return np.zeros((rows, cols), np.float32)


def gather_matrices(cols_here):
    windows = cols_here // WLON
    own_cols = cols_here - SHIFT_LON
    own = place(windows * WLAT * WLON, WLAT * cols_here)
    lat = place(windows * WLAT * WLON, SHIFT_LAT * own_cols)
    corner = place(windows * WLAT * WLON, WLAT * SHIFT_LON)
    for n in range(windows):
        for a in range(WLAT):
            for x in range(WLON):
                row = (n * WLAT + a) * WLON + x
                col = n * WLON + x
                if col < own_cols:
                    if a < SHIFT_LAT:
                        own[row, (a + SHIFT_LAT) * cols_here + col + SHIFT_LON] = 1
                    else:
                        lat[row, (a - SHIFT_LAT) * own_cols + col] = 1
                else:
                    corner[row, a * SHIFT_LON + col - own_cols] = 1
    return own, lat, corner


def scatter_matrices(cols_here):
    own_cols = cols_here - SHIFT_LON
    lat = place(WLAT * cols_here, SHIFT_LAT * own_cols)
    corner = place(WLAT * cols_here, WLAT * SHIFT_LON)
    for a in range(WLAT):
        for c in range(cols_here):
            row = a * cols_here + c
            if c >= SHIFT_LON:
                if a < SHIFT_LAT:
                    lat[row, a * own_cols + c - SHIFT_LON] = 1
            elif a >= SHIFT_LAT:
                corner[row, (a - SHIFT_LAT) * SHIFT_LON + c] = 1
            else:
                corner[row, (a + SHIFT_LAT) * SHIFT_LON + c] = 1
    return lat, corner


def lon_selectors():
    out = np.zeros((WLON, 3 * LANES, 2 * LANES), np.float32)
    for xj in range(WLON):
        for g in range(GROUPS):
            for xi in range(WLON):
                out[xj, g * SPAN + xi - xj + WLON - 1, g * WLON + xi] = 1
    return out


def dot(a, b, ca=1, cb=0):
    return lax.dot_general(a, b, (((ca,), (cb,)), ((), ())), preferred_element_type=F32)


def split(value):
    high = value.astype(BF)
    return high, (value - high.astype(F32)).astype(BF)


def prep_kernel(wx_ref, gx_ref, lat_pick, lon_pick, diag_pick, lat_out, lon_out, diag_out):
    def step(level, carry):
        for pick, strip in ((lat_pick, lat_out), (lon_pick, lon_out), (diag_pick, diag_out)):
            strip[level] = jnp.concatenate(
                [dot(pick[...], ref[level]) for ref in (wx_ref, gx_ref)], axis=1
            ).astype(BF)
        return carry

    lax.fori_loop(0, wx_ref.shape[0], step, 0, unroll=True)


def expand_kernel(last_ref, table_ref, sel_ref, bias_ref, flat_s, block_s, table_s):
    pairs, _, entries = table_ref.shape
    levs = pairs // HEADS
    for h in range(HEADS):
        for lev in range(levs):
            r = h * levs + lev
            flat_s[r : r + 1, :entries] = table_ref[lev * HEADS + h]
    for m in range(GROUPS):
        z_j, a_j = divmod(m, WLAT)
        for g in range(GROUPS):
            z_i, a_i = divmod(g, WLAT)
            at = SPAN * (((z_i * WLEV + z_j) * WLAT + a_i) * WLAT + a_j)
            block_s[m, :, g * SPAN : (g + 1) * SPAN] = flat_s[:, at : at + SPAN]
        for j in range(3):
            table_s[j, pl.ds(m, pairs, stride=GROUPS), :] = block_s[m, :, j * LANES : (j + 1) * LANES]
    table = jnp.concatenate([table_s[j] for j in range(3)], axis=1)[:, : GROUPS * SPAN]
    high, low = split(table)
    rows = levs * GROUPS
    row_id = lax.broadcasted_iota(jnp.int32, (BIAS_ROWS, TOK), 0)
    col_id = lax.broadcasted_iota(jnp.int32, (BIAS_ROWS, TOK), 1)
    m_j = row_id % GROUPS
    lev = row_id // GROUPS % levs
    a_i = col_id // WLON % WLAT
    z_i = col_id // (WLON * WLAT)
    cross_lev = jnp.logical_and(lev == levs - 1, m_j // WLAT != z_i)
    cross_lat = jnp.logical_and(last_ref[0] == 1, (m_j % WLAT >= SHIFT_LAT) != (a_i >= SHIFT_LAT))
    hide = jnp.where(jnp.logical_or(cross_lev, cross_lat), MASKED, 0.0)
    pad = jnp.zeros((rows, HLANES - HEADS * TOK), F32)
    for xj in range(WLON):
        sel = sel_ref[xj, : GROUPS * SPAN, :TOK]
        value = dot(high, sel) + dot(low, sel) + hide
        wide = jnp.concatenate([value[h * rows : (h + 1) * rows] for h in range(HEADS)] + [pad], axis=1)
        for t in range(HTILES):
            bias_ref[t, pl.ds(xj, rows, stride=WLON), :] = wide[:, t * LANES : (t + 1) * LANES]


def main_kernel(
    core_ref, wx_ref, gx_ref, lat_in, lon_in, diag_in, gain_ref, wqkv_ref, proj_ref,
    pown_ref, plat_ref, plon_ref, pdiag_ref, bias_hbm, sel_hbm,
    att_ref, gi_ref, keep_ref, send_ref,
    x_s, g_s, normed_s, inv_s, q_s, k_s, v_s, da_s, dq_s, dk_s, dv_s, hid_t, dsum_s, pay_s, bias_s, sel_s, sems,
):
    bias_copy = pltpu.make_async_copy(bias_hbm, bias_s, sems.at[0])
    sel_copy = pltpu.make_async_copy(sel_hbm, sel_s, sems.at[1])
    bias_copy.start()
    sel_copy.start()
    levels = wx_ref.shape[0]
    half = TOK // 2
    windows = x_s.shape[0] // TOK
    for level in range(levels):
        back = (level + levels - 1) % levels
        k, z = back // WLEV, back % WLEV
        place_own = pown_ref[...]
        strips = ((plat_ref, lat_in), (plon_ref, lon_in), (pdiag_ref, diag_in))
        xw = dot(place_own, wx_ref[level])
        gw = dot(place_own, gx_ref[level])
        for where_ref, strip in strips:
            both = strip[level]
            xw = xw + dot(where_ref[...], both[:, :CH])
            gw = gw + dot(where_ref[...], both[:, CH:])
        for n in range(2):
            at = (2 * k + n) * TOK + z * half
            x_s[at : at + half, :] = xw[n * half : (n + 1) * half]
            g_s[at : at + half, :] = gw[n * half : (n + 1) * half]

    gain = gain_ref[...]
    inv_root = HD ** (-0.5)

    def eye(n):
        return (lax.broadcasted_iota(jnp.int32, (n, n), 0) == lax.broadcasted_iota(jnp.int32, (n, n), 1)).astype(F32).astype(BF)

    eye_c = eye(CH)
    eye_t = eye(TOK)
    chunks = [slice(at, at + CHUNK) for at in range(0, x_s.shape[0], CHUNK)]
    for rows in chunks:
        x = x_s[rows]
        centred = x - jnp.mean(x, axis=-1, keepdims=True)
        inv_std = lax.rsqrt(jnp.mean(centred * centred, axis=-1, keepdims=True) + EPSILON)
        normed = centred * inv_std
        normed_s[rows] = normed
        inv_s[rows] = jnp.broadcast_to(inv_std, (CHUNK, LANES))
        hidden = (normed * gain).astype(BF)
        q_s[rows] = (dot(hidden, wqkv_ref[0]) * inv_root).astype(BF)
        k_s[rows] = dot(hidden, wqkv_ref[1]).astype(BF)
        v_s[rows] = dot(hidden, wqkv_ref[2]).astype(BF)
        da_s[rows] = dot(g_s[rows].astype(BF), proj_ref[...], 1, 1).astype(BF)
        hid_t[:, rows] = dot(eye_c, hidden, 1, 1).astype(BF)

    channel = lax.broadcasted_iota(jnp.int32, (TOK, CH), 1)
    head_mask = [jnp.logical_and(channel >= h * HD, channel < (h + 1) * HD) for h in range(HEADS)]
    zero = jnp.zeros((TOK, CH), BF)
    tail = jnp.zeros((HLANES - HEADS * TOK, CH), BF)

    def per_head(value):
        return jnp.concatenate([jnp.where(mask, value, zero) for mask in head_mask] + [tail], axis=0)

    bias_copy.wait()
    gproj = jnp.zeros((CH, CH), F32)
    for w in range(windows):
        rows = slice(w * TOK, (w + 1) * TOK)
        first = w % 2 == 0
        lev_rows = slice(w // 2 * TOK, (w // 2 + 1) * TOK)
        key, v = k_s[rows], v_s[rows]
        q_heads = per_head(q_s[rows])
        da_heads = per_head(da_s[rows])
        key_t = dot(eye_c, key, 1, 1).astype(BF)
        v_t = dot(eye_c, v, 1, 1).astype(BF)
        scores = dot(key, q_heads, 1, 1)
        scores = scores + jnp.concatenate([bias_s[t, lev_rows, :] for t in range(HTILES)], axis=1)
        dp = dot(v, da_heads, 1, 1)
        e = jnp.exp(scores - jnp.max(scores, axis=0, keepdims=True))
        probs = (e * (1.0 / jnp.sum(e, axis=0, keepdims=True))).astype(BF)
        dv_s[rows] = dot(probs, da_heads).astype(BF)
        pf = probs.astype(F32)
        t_prod = pf * dp
        ds = t_prod - pf * jnp.sum(t_prod, axis=0, keepdims=True)
        dsb = ds.astype(BF)
        for t in range(HTILES):
            part = ds[:, t * LANES : (t + 1) * LANES]
            dsum_s[t, lev_rows, :] = part if first else dsum_s[t, lev_rows, :] + part
        dk_s[rows] = dot(dsb, q_heads).astype(BF)
        att_t = jnp.concatenate(
            [dot(v_t[h * HD : (h + 1) * HD], probs[:, h * TOK : (h + 1) * TOK]) for h in range(HEADS)], axis=0
        ).astype(BF)
        dq_t = jnp.concatenate(
            [dot(key_t[h * HD : (h + 1) * HD], dsb[:, h * TOK : (h + 1) * TOK]) for h in range(HEADS)], axis=0
        )
        dq_t = (dq_t * inv_root).astype(BF)
        att_ref[rows] = dot(eye_t, att_t, 1, 1).astype(BF)
        dq_s[rows] = dot(eye_t, dq_t, 1, 1).astype(BF)
        gproj = gproj + dot(att_t, g_s[rows].astype(BF))

    g_gain = jnp.zeros((1, CH), F32)
    for rows in chunks:
        gh = (
            dot(dq_s[rows], wqkv_ref[0], 1, 1)
            + dot(dk_s[rows], wqkv_ref[1], 1, 1)
            + dot(dv_s[rows], wqkv_ref[2], 1, 1)
        )
        normed = normed_s[rows]
        g_gain = g_gain + jnp.sum(gh * normed, axis=0, keepdims=True)
        gn = gh * gain
        gi = inv_s[rows][:, :1] * (
            gn
            - jnp.mean(gn, axis=-1, keepdims=True)
            - normed * jnp.mean(gn * normed, axis=-1, keepdims=True)
        )
        gi_ref[rows] = gi.astype(BF)

    g_wide = [dot(hid_t[...], part[...]) for part in (dq_s, dk_s, dv_s)]
    weights = jnp.concatenate(g_wide + [gproj], axis=1)
    for j in range(WTILES):
        pay_s[j * CH : (j + 1) * CH, :] = weights[:, j * LANES : (j + 1) * LANES]
    pay_s[GROW:, :] = jnp.zeros((PAY - GROW, LANES), F32)
    pay_s[GROW : GROW + 1, :] = g_gain[:, :LANES]
    pay_s[GROW + 1 : GROW + 2, : CH - LANES] = g_gain[:, LANES:]

    sel_copy.wait()
    lev_groups = dsum_s.shape[1] // WLON
    g_bias = jnp.zeros((BIAS_ROWS, 3 * LANES), F32)
    for xj in range(WLON):
        wide = jnp.concatenate(
            [dsum_s[t, pl.ds(xj, lev_groups, stride=WLON), :] for t in range(HTILES)], axis=1
        ).astype(BF)
        stacked = jnp.concatenate([wide[:, h * TOK : (h + 1) * TOK] for h in range(HEADS)], axis=0)
        g_bias = g_bias + dot(stacked, sel_s[xj, :, :TOK], 1, 1)
    for j in range(3):
        pay_s[BROW + j * BIAS_ROWS : BROW + (j + 1) * BIAS_ROWS, :] = g_bias[:, j * LANES : (j + 1) * LANES]
    core = core_ref[0]
    half_rows = PAY // 2
    keep_ref[...] = pay_s[pl.ds(pl.multiple_of(core * half_rows, half_rows), half_rows), :].astype(BF)
    send_ref[...] = pay_s[pl.ds(pl.multiple_of((1 - core) * half_rows, half_rows), half_rows), :].astype(BF)


def return_kernel(
    wx_ref, gx_ref, att_ref, gi_ref, proj_ref, pown_ref, plat_ref, plon_ref, pdiag_ref,
    base_ref, gbase_ref, lat_out, lon_out, diag_out, br_s, gi_s,
):
    br_s[...] = dot(att_ref[...], proj_ref[...])
    gi_s[...] = gi_ref[...].astype(F32)
    levels = wx_ref.shape[0]
    half = TOK // 2
    for level in range(levels):
        back = (level + levels - 1) % levels
        k, z = back // WLEV, back % WLEV
        moved = []
        for src, own_in, own_out in ((br_s, wx_ref, base_ref), (gi_s, gx_ref, gbase_ref)):
            starts = [(2 * k + n) * TOK + z * half for n in range(2)]
            rows = jnp.concatenate([src[at : at + half, :] for at in starts], axis=0).astype(BF)
            own_out[level] = (own_in[level].astype(F32) + dot(pown_ref[...], rows, 0, 0)).astype(BF)
            moved.append(rows)
        for where_ref, strip in ((plat_ref, lat_out), (plon_ref, lon_out), (pdiag_ref, diag_out)):
            strip[level] = jnp.concatenate(
                [dot(where_ref[...], rows, 0, 0) for rows in moved], axis=1
            ).astype(BF)


def add_kernel(base_ref, gbase_ref, lat_in, lon_in, diag_in, slat_ref, slon_ref, sdiag_ref, out_ref, gout_ref):
    for level in range(base_ref.shape[0]):
        up = base_ref[level].astype(F32)
        gup = gbase_ref[level].astype(F32)
        for where_ref, strip in ((slat_ref, lat_in), (slon_ref, lon_in), (sdiag_ref, diag_in)):
            both = strip[level]
            up = up + dot(where_ref[...], both[:, :CH])
            gup = gup + dot(where_ref[...], both[:, CH:])
        out_ref[level] = up.astype(BF)
        gout_ref[level] = gup.astype(BF)


def finish_kernel(
    factor, core_ref, mine_ref, other_ref, gqkv_ref, gproj_ref, ggain_ref, gbias_ref, full_s, table_s,
):
    core = core_ref[0]
    half_rows = PAY // 2
    full_s[pl.ds(pl.multiple_of(core * half_rows, half_rows), half_rows), :] = mine_ref[...].astype(F32) * factor
    full_s[pl.ds(pl.multiple_of((1 - core) * half_rows, half_rows), half_rows), :] = other_ref[...].astype(F32) * factor
    tiles = [full_s[j * CH : (j + 1) * CH, :] for j in range(WTILES)]
    for j in range(4):
        gqkv_ref[:, j * LANES : (j + 1) * LANES] = tiles[j]
    cut = 3 * CH - 4 * LANES
    gqkv_ref[:, 4 * LANES :] = tiles[4][:, :cut]
    gproj_ref[...] = jnp.concatenate([tiles[4][:, cut:], tiles[5]], axis=1)
    ggain_ref[...] = jnp.concatenate(
        [full_s[GROW : GROW + 1, :], full_s[GROW + 1 : GROW + 2, : CH - LANES]], axis=1
    )
    pairs = BIAS_ROWS // GROUPS
    levs = pairs // HEADS
    for m in range(GROUPS):
        z_j, a_j = divmod(m, WLAT)
        block = jnp.concatenate(
            [full_s[pl.ds(BROW + j * BIAS_ROWS + m, pairs, stride=GROUPS), :] for j in range(3)], axis=1
        )
        for g in range(GROUPS):
            z_i, a_i = divmod(g, WLAT)
            to = SPAN * (((z_i * WLEV + z_j) * WLAT + a_i) * WLAT + a_j)
            table_s[:, to : to + SPAN] = block[:, g * SPAN : (g + 1) * SPAN]
    for h in range(HEADS):
        for lev in range(levs):
            r = h * levs + lev
            gbias_ref[lev * HEADS + h] = table_s[r : r + 1, : gbias_ref.shape[2]]


def passed(value, lat_step, lon_step):
    lats, highs, zs = lax.axis_size("lat"), lax.axis_size("yhi"), lax.axis_size("z")
    lons = highs * zs
    pairs = [
        (b * lats + a, (b + lon_step) % lons * lats + (a + lat_step) % lats)
        for b in range(lons)
        for a in range(lats)
    ]
    return lax.ppermute(value, ("yhi", "z", "lat"), pairs)


def swapped(value):
    return lax.ppermute(value, "core", [(0, 1), (1, 0)])


def total_over_devices(keep, send, between, last):
    wide = ("ylo", "yhi", "z")
    peers = lax.axis_size("ylo") * lax.axis_size("yhi") * lax.axis_size("z")
    half = (keep.astype(F32) + swapped(send).astype(F32)).astype(BF)
    inputs, fn = between
    half, inputs = lax.optimization_barrier((half, inputs))
    pieces = lax.all_to_all(half, wide, 0, 0, tiled=True)
    keeps, strips = fn(inputs)
    pieces, _ = lax.optimization_barrier((pieces, strips))
    piece = jnp.sum(pieces.reshape(peers, PIECE, LANES).astype(F32), axis=0)
    lats = lax.axis_size("lat")
    place_here = lax.axis_index("core") * peers + lax.axis_index(wide)
    shared = jnp.logical_or(place_here < BROW // PIECE, place_here >= GROW // PIECE)
    others = jnp.zeros_like(piece)
    for step in range(1, lats):
        others = others + lax.ppermute(piece, "lat", [(a, (a + step) % lats) for a in range(lats)])
    piece = jnp.where(shared, piece + others, piece).astype(BF)
    spread = jnp.broadcast_to(piece[None], (peers, PIECE, LANES)).reshape(half.shape)
    spread, strips = lax.optimization_barrier((spread, strips))
    backs = [passed(strip, *step) for strip, step in zip(strips, ((1, 0), (0, 1), (1, 1)))]
    mine = lax.all_to_all(spread, wide, 0, 0, tiled=True)
    mine, backs = lax.optimization_barrier((mine, backs))
    return mine, swapped(mine), last(*keeps, *backs)


def call(kernel, out_shape, scratch=(), smem=0, count=0, flops=0, far=0):
    specs = [pl.BlockSpec(memory_space=pltpu.SMEM)] * smem
    specs += [pl.BlockSpec(memory_space=pltpu.VMEM)] * (count - smem - far)
    specs += [pl.BlockSpec(memory_space=pl.ANY)] * far
    return pl.pallas_call(
        kernel,
        out_shape=out_shape,
        in_specs=specs,
        out_specs=jax.tree.map(lambda _: pl.BlockSpec(memory_space=pltpu.VMEM), out_shape),
        scratch_shapes=list(scratch),
        compiler_params=pltpu.CompilerParams(vmem_limit_bytes=VMEM_LIMIT),
        cost_estimate=pl.CostEstimate(flops=flops, bytes_accessed=flops // 500, transcendentals=0),
    )


def sds(shape, dtype):
    return jax.ShapeDtypeStruct(shape, dtype)


def shards(weather, cotangent, norm_gain, qkv_weight, proj_weight, bias_table):
    samples, levels, rows_here, cols_here, channels = weather.shape
    lat_index = lax.axis_index("lat")
    lat_count = lax.axis_size("lat")
    plane = rows_here * cols_here
    own_cols = cols_here - SHIFT_LON
    wx = weather.reshape(levels, plane, CH)
    gx = cotangent.reshape(levels, plane, CH)
    edge = SHIFT_LAT * SHIFT_LON
    lat_shape = sds((levels, SHIFT_LAT * own_cols, 2 * CH), BF)
    edge_shape = sds((levels, edge, 2 * CH), BF)
    slat, scor = scatter_matrices(cols_here)
    scatter = (slat, scor[:, :edge], scor[:, edge:])
    strips = call(prep_kernel, (lat_shape, edge_shape, edge_shape), count=5, flops=10**9)(
        wx, gx, *[jnp.asarray(m.T, BF) for m in scatter]
    )
    lat_in = passed(strips[0], -1, 0)
    lon_in = passed(strips[1], 0, -1)
    diag_in = passed(strips[2], -1, -1)

    lev_windows = bias_table.shape[0]
    pairs = lev_windows * HEADS
    entries = bias_table.shape[-1]
    table = bias_table.transpose(0, 2, 1, 3).reshape(pairs, 1, entries)
    last = (lat_index == lat_count - 1).astype(jnp.int32).reshape(1)
    sel = jnp.asarray(lon_selectors(), BF)
    bias_rows = lev_windows * TOK
    flat_shape = pltpu.VMEM((pairs, -(-entries // LANES) * LANES), F32)
    bias_shape = (HTILES, bias_rows, LANES)
    bias = call(
        expand_kernel,
        sds(bias_shape, F32),
        scratch=[flat_shape, pltpu.VMEM((GROUPS, pairs, 3 * LANES), F32), pltpu.VMEM((3, BIAS_ROWS, LANES), F32)],
        smem=1, count=3, flops=10**9,
    )(last, table, sel)

    own_m, lat_m, corner_m = gather_matrices(cols_here)
    mats = [jnp.asarray(m, BF) for m in (own_m, lat_m, corner_m[:, :edge], corner_m[:, edge:])]
    wqkv = qkv_weight.reshape(CH, 3, CH).transpose(1, 0, 2)
    tokens = levels * plane
    plane_shape = sds((levels, plane, CH), BF)
    token_shape = sds((tokens, CH), BF)
    core = lax.axis_index("core").astype(jnp.int32).reshape(1)
    half_shape = sds((PAY // 2, LANES), BF)
    wide_f = pltpu.VMEM((tokens, CH), F32)
    wide_b = pltpu.VMEM((tokens, CH), BF)
    att, gi, keep, send = call(
        main_kernel,
        (token_shape, token_shape, half_shape, half_shape),
        scratch=[wide_f, wide_f, wide_f, pltpu.VMEM((tokens, LANES), F32)]
        + [wide_b] * 7
        + [
            pltpu.VMEM((CH, tokens), BF),
            pltpu.VMEM(bias_shape, F32),
            pltpu.VMEM((PAY, LANES), F32),
            pltpu.VMEM(bias_shape, F32),
            pltpu.VMEM(sel.shape, BF),
            pltpu.SemaphoreType.DMA((2,)),
        ],
        smem=1,
        count=15,
        far=2,
        flops=10**10,
    )(core, wx, gx, lat_in, lon_in, diag_in, norm_gain.reshape(1, CH), wqkv, proj_weight, *mats, bias, sel)

    def give_back(inputs):
        base, gbase, *strips = call(
            return_kernel,
            (plane_shape, plane_shape, lat_shape, edge_shape, edge_shape),
            scratch=[wide_f, wide_f],
            count=9,
            flops=2 * 10**9,
        )(wx, gx, *inputs, proj_weight, *mats)
        return (base, gbase), strips

    def add_up(*parts):
        return call(add_kernel, (plane_shape, plane_shape), count=8, flops=2 * 10**9)(
            *parts, *[jnp.asarray(m, BF) for m in scatter]
        )

    mine, other, (out, gout) = total_over_devices(keep, send, ((att, gi), give_back), add_up)
    factor = (samples * levels * rows_here * cols_here * lax.axis_size(("ylo", "core", "yhi", "z", "lat"))) ** (-0.5)
    gqkv, gproj, ggain, gbias = call(
        functools.partial(finish_kernel, factor),
        (sds(qkv_weight.shape, F32), sds(proj_weight.shape, F32), sds((1, CH), F32), sds((pairs, 1, entries), F32)),
        scratch=[pltpu.VMEM((PAY, LANES), F32), flat_shape],
        smem=1,
        count=3,
        flops=10**9,
    )(core, mine, other)
    return (
        out.reshape(weather.shape),
        gout.reshape(weather.shape),
        gqkv,
        gproj,
        ggain.reshape(CH),
        gbias.reshape(lev_windows, HEADS, 1, entries).transpose(0, 2, 1, 3),
    )


def solution(mesh):
    fine = jax.sharding.Mesh(mesh.devices.reshape(2, 2, 2, 8, 4), ("ylo", "core", "yhi", "z", "lat"))
    dp, lon = ("ylo", "core"), ("yhi", "z")
    grid = P(dp, None, "lat", lon, None)
    table = P(None, "lat", None, None)
    return jax.shard_map(
        shards,
        mesh=fine,
        in_specs=(grid, grid, P(), P(), P(), table),
        out_specs=(grid, grid, P(), P(), P(), table),
        check_vma=False,
    )
```

```python
import functools

import numpy as np
import jax
import jax.numpy as jnp
from jax import lax
from jax.experimental import pallas as pl
from jax.experimental.pallas import tpu as pltpu
from jax.sharding import PartitionSpec as P

HEADS = 6
WLEV = 2
WLAT = 6
WLON = 12
HD = 32
CH = 192
TOK = 144
LANES = 128
SHIFT_LAT = 3
SHIFT_LON = 6
SPAN = 2 * WLON - 1
GROUPS = WLEV * WLAT
MASKED = -1e30
EPSILON = 1e-05
BF = jnp.bfloat16
F32 = jnp.float32
PAY = 2048
WTILES = 6
BIAS_ROWS = 288
BROW = WTILES * CH
GROW = BROW + 3 * BIAS_ROWS
PIECE = 32
HTILES = 7
HLANES = HTILES * LANES
CHUNK = 3 * LANES
VMEM_LIMIT = 56 * 1024 * 1024


def place(rows, cols):
    return np.zeros((rows, cols), np.float32)


def gather_matrices(cols_here):
    windows = cols_here // WLON
    own_cols = cols_here - SHIFT_LON
    own = place(windows * WLAT * WLON, WLAT * cols_here)
    lat = place(windows * WLAT * WLON, SHIFT_LAT * own_cols)
    corner = place(windows * WLAT * WLON, WLAT * SHIFT_LON)
    for n in range(windows):
        for a in range(WLAT):
            for x in range(WLON):
                row = (n * WLAT + a) * WLON + x
                col = n * WLON + x
                if col < own_cols:
                    if a < SHIFT_LAT:
                        own[row, (a + SHIFT_LAT) * cols_here + col + SHIFT_LON] = 1
                    else:
                        lat[row, (a - SHIFT_LAT) * own_cols + col] = 1
                else:
                    corner[row, a * SHIFT_LON + col - own_cols] = 1
    return own, lat, corner


def scatter_matrices(cols_here):
    own_cols = cols_here - SHIFT_LON
    lat = place(WLAT * cols_here, SHIFT_LAT * own_cols)
    corner = place(WLAT * cols_here, WLAT * SHIFT_LON)
    for a in range(WLAT):
        for c in range(cols_here):
            row = a * cols_here + c
            if c >= SHIFT_LON:
                if a < SHIFT_LAT:
                    lat[row, a * own_cols + c - SHIFT_LON] = 1
            elif a >= SHIFT_LAT:
                corner[row, (a - SHIFT_LAT) * SHIFT_LON + c] = 1
            else:
                corner[row, (a + SHIFT_LAT) * SHIFT_LON + c] = 1
    return lat, corner


def lon_selectors():
    out = np.zeros((WLON, 3 * LANES, 2 * LANES), np.float32)
    for xj in range(WLON):
        for g in range(GROUPS):
            for xi in range(WLON):
                out[xj, g * SPAN + xi - xj + WLON - 1, g * WLON + xi] = 1
    return out


def dot(a, b, ca=1, cb=0):
    return lax.dot_general(a, b, (((ca,), (cb,)), ((), ())), preferred_element_type=F32)


def split(value):
    high = value.astype(BF)
    return high, (value - high.astype(F32)).astype(BF)


def prep_kernel(wx_ref, gx_ref, lat_pick, lon_pick, diag_pick, lat_out, lon_out, diag_out):
    def step(level, carry):
        for pick, strip in ((lat_pick, lat_out), (lon_pick, lon_out), (diag_pick, diag_out)):
            strip[level] = jnp.concatenate(
                [dot(pick[...], ref[level]) for ref in (wx_ref, gx_ref)], axis=1
            ).astype(BF)
        return carry

    lax.fori_loop(0, wx_ref.shape[0], step, 0, unroll=True)


def expand_kernel(last_ref, table_ref, sel_ref, bias_ref, flat_s, block_s, table_s):
    pairs, _, entries = table_ref.shape
    levs = pairs // HEADS
    for h in range(HEADS):
        for lev in range(levs):
            r = h * levs + lev
            flat_s[r : r + 1, :entries] = table_ref[lev * HEADS + h]
    for m in range(GROUPS):
        z_j, a_j = divmod(m, WLAT)
        for g in range(GROUPS):
            z_i, a_i = divmod(g, WLAT)
            at = SPAN * (((z_i * WLEV + z_j) * WLAT + a_i) * WLAT + a_j)
            block_s[m, :, g * SPAN : (g + 1) * SPAN] = flat_s[:, at : at + SPAN]
        for j in range(3):
            table_s[j, pl.ds(m, pairs, stride=GROUPS), :] = block_s[m, :, j * LANES : (j + 1) * LANES]
    table = jnp.concatenate([table_s[j] for j in range(3)], axis=1)[:, : GROUPS * SPAN]
    high, low = split(table)
    rows = levs * GROUPS
    row_id = lax.broadcasted_iota(jnp.int32, (BIAS_ROWS, TOK), 0)
    col_id = lax.broadcasted_iota(jnp.int32, (BIAS_ROWS, TOK), 1)
    m_j = row_id % GROUPS
    lev = row_id // GROUPS % levs
    a_i = col_id // WLON % WLAT
    z_i = col_id // (WLON * WLAT)
    cross_lev = jnp.logical_and(lev == levs - 1, m_j // WLAT != z_i)
    cross_lat = jnp.logical_and(last_ref[0] == 1, (m_j % WLAT >= SHIFT_LAT) != (a_i >= SHIFT_LAT))
    hide = jnp.where(jnp.logical_or(cross_lev, cross_lat), MASKED, 0.0)
    pad = jnp.zeros((rows, HLANES - HEADS * TOK), F32)
    for xj in range(WLON):
        sel = sel_ref[xj, : GROUPS * SPAN, :TOK]
        value = dot(high, sel) + dot(low, sel) + hide
        wide = jnp.concatenate([value[h * rows : (h + 1) * rows] for h in range(HEADS)] + [pad], axis=1)
        for t in range(HTILES):
            bias_ref[t, pl.ds(xj, rows, stride=WLON), :] = wide[:, t * LANES : (t + 1) * LANES]


def main_kernel(
    core_ref, wx_ref, gx_ref, lat_in, lon_in, diag_in, gain_ref, wqkv_ref, proj_ref,
    pown_ref, plat_ref, plon_ref, pdiag_ref, bias_hbm, sel_hbm,
    att_ref, gi_ref, keep_ref, send_ref,
    x_s, g_s, normed_s, inv_s, q_s, k_s, v_s, da_s, dq_s, dk_s, dv_s, hid_t, dsum_s, pay_s, bias_s, sel_s, sems,
):
    bias_copy = pltpu.make_async_copy(bias_hbm, bias_s, sems.at[0])
    sel_copy = pltpu.make_async_copy(sel_hbm, sel_s, sems.at[1])
    bias_copy.start()
    sel_copy.start()
    levels = wx_ref.shape[0]
    half = TOK // 2
    windows = x_s.shape[0] // TOK
    for level in range(levels):
        back = (level + levels - 1) % levels
        k, z = back // WLEV, back % WLEV
        place_own = pown_ref[...]
        strips = ((plat_ref, lat_in), (plon_ref, lon_in), (pdiag_ref, diag_in))
        xw = dot(place_own, wx_ref[level])
        gw = dot(place_own, gx_ref[level])
        for where_ref, strip in strips:
            both = strip[level]
            xw = xw + dot(where_ref[...], both[:, :CH])
            gw = gw + dot(where_ref[...], both[:, CH:])
        for n in range(2):
            at = (2 * k + n) * TOK + z * half
            x_s[at : at + half, :] = xw[n * half : (n + 1) * half]
            g_s[at : at + half, :] = gw[n * half : (n + 1) * half]

    gain = gain_ref[...]
    inv_root = HD ** (-0.5)

    def eye(n):
        return (lax.broadcasted_iota(jnp.int32, (n, n), 0) == lax.broadcasted_iota(jnp.int32, (n, n), 1)).astype(F32).astype(BF)

    eye_c = eye(CH)
    eye_t = eye(TOK)
    chunks = [slice(at, at + CHUNK) for at in range(0, x_s.shape[0], CHUNK)]
    for rows in chunks:
        x = x_s[rows]
        centred = x - jnp.mean(x, axis=-1, keepdims=True)
        inv_std = lax.rsqrt(jnp.mean(centred * centred, axis=-1, keepdims=True) + EPSILON)
        normed = centred * inv_std
        normed_s[rows] = normed
        inv_s[rows] = jnp.broadcast_to(inv_std, (CHUNK, LANES))
        hidden = (normed * gain).astype(BF)
        q_s[rows] = (dot(hidden, wqkv_ref[0]) * inv_root).astype(BF)
        k_s[rows] = dot(hidden, wqkv_ref[1]).astype(BF)
        v_s[rows] = dot(hidden, wqkv_ref[2]).astype(BF)
        da_s[rows] = dot(g_s[rows].astype(BF), proj_ref[...], 1, 1).astype(BF)
        hid_t[:, rows] = dot(eye_c, hidden, 1, 1).astype(BF)

    channel = lax.broadcasted_iota(jnp.int32, (TOK, CH), 1)
    head_mask = [jnp.logical_and(channel >= h * HD, channel < (h + 1) * HD) for h in range(HEADS)]
    zero = jnp.zeros((TOK, CH), BF)
    tail = jnp.zeros((HLANES - HEADS * TOK, CH), BF)

    def per_head(value):
        return jnp.concatenate([jnp.where(mask, value, zero) for mask in head_mask] + [tail], axis=0)

    bias_copy.wait()
    gproj = jnp.zeros((CH, CH), F32)
    for w in range(windows):
        rows = slice(w * TOK, (w + 1) * TOK)
        first = w % 2 == 0
        lev_rows = slice(w // 2 * TOK, (w // 2 + 1) * TOK)
        key, v = k_s[rows], v_s[rows]
        q_heads = per_head(q_s[rows])
        da_heads = per_head(da_s[rows])
        key_t = dot(eye_c, key, 1, 1).astype(BF)
        v_t = dot(eye_c, v, 1, 1).astype(BF)
        scores = dot(key, q_heads, 1, 1)
        scores = scores + jnp.concatenate([bias_s[t, lev_rows, :] for t in range(HTILES)], axis=1)
        dp = dot(v, da_heads, 1, 1)
        e = jnp.exp(scores - jnp.max(scores, axis=0, keepdims=True))
        probs = (e * (1.0 / jnp.sum(e, axis=0, keepdims=True))).astype(BF)
        dv_s[rows] = dot(probs, da_heads).astype(BF)
        pf = probs.astype(F32)
        t_prod = pf * dp
        ds = t_prod - pf * jnp.sum(t_prod, axis=0, keepdims=True)
        dsb = ds.astype(BF)
        for t in range(HTILES):
            part = ds[:, t * LANES : (t + 1) * LANES]
            dsum_s[t, lev_rows, :] = part if first else dsum_s[t, lev_rows, :] + part
        dk_s[rows] = dot(dsb, q_heads).astype(BF)
        att_t = jnp.concatenate(
            [dot(v_t[h * HD : (h + 1) * HD], probs[:, h * TOK : (h + 1) * TOK]) for h in range(HEADS)], axis=0
        ).astype(BF)
        dq_t = jnp.concatenate(
            [dot(key_t[h * HD : (h + 1) * HD], dsb[:, h * TOK : (h + 1) * TOK]) for h in range(HEADS)], axis=0
        )
        dq_t = (dq_t * inv_root).astype(BF)
        att_ref[rows] = dot(eye_t, att_t, 1, 1).astype(BF)
        dq_s[rows] = dot(eye_t, dq_t, 1, 1).astype(BF)
        gproj = gproj + dot(att_t, g_s[rows].astype(BF))

    g_gain = jnp.zeros((1, CH), F32)
    for rows in chunks:
        gh = (
            dot(dq_s[rows], wqkv_ref[0], 1, 1)
            + dot(dk_s[rows], wqkv_ref[1], 1, 1)
            + dot(dv_s[rows], wqkv_ref[2], 1, 1)
        )
        normed = normed_s[rows]
        g_gain = g_gain + jnp.sum(gh * normed, axis=0, keepdims=True)
        gn = gh * gain
        gi = inv_s[rows][:, :1] * (
            gn
            - jnp.mean(gn, axis=-1, keepdims=True)
            - normed * jnp.mean(gn * normed, axis=-1, keepdims=True)
        )
        gi_ref[rows] = gi.astype(BF)

    g_wide = [dot(hid_t[...], part[...]) for part in (dq_s, dk_s, dv_s)]
    weights = jnp.concatenate(g_wide + [gproj], axis=1)
    for j in range(WTILES):
        pay_s[j * CH : (j + 1) * CH, :] = weights[:, j * LANES : (j + 1) * LANES]
    pay_s[GROW:, :] = jnp.zeros((PAY - GROW, LANES), F32)
    pay_s[GROW : GROW + 1, :] = g_gain[:, :LANES]
    pay_s[GROW + 1 : GROW + 2, : CH - LANES] = g_gain[:, LANES:]

    sel_copy.wait()
    lev_groups = dsum_s.shape[1] // WLON
    g_bias = jnp.zeros((BIAS_ROWS, 3 * LANES), F32)
    for xj in range(WLON):
        wide = jnp.concatenate(
            [dsum_s[t, pl.ds(xj, lev_groups, stride=WLON), :] for t in range(HTILES)], axis=1
        ).astype(BF)
        stacked = jnp.concatenate([wide[:, h * TOK : (h + 1) * TOK] for h in range(HEADS)], axis=0)
        g_bias = g_bias + dot(stacked, sel_s[xj, :, :TOK], 1, 1)
    for j in range(3):
        pay_s[BROW + j * BIAS_ROWS : BROW + (j + 1) * BIAS_ROWS, :] = g_bias[:, j * LANES : (j + 1) * LANES]
    core = core_ref[0]
    half_rows = PAY // 2
    keep_ref[...] = pay_s[pl.ds(pl.multiple_of(core * half_rows, half_rows), half_rows), :].astype(BF)
    send_ref[...] = pay_s[pl.ds(pl.multiple_of((1 - core) * half_rows, half_rows), half_rows), :].astype(BF)


def return_kernel(
    wx_ref, gx_ref, att_ref, gi_ref, proj_ref, pown_ref, plat_ref, plon_ref, pdiag_ref,
    base_ref, gbase_ref, lat_out, lon_out, diag_out, br_s, gi_s,
):
    br_s[...] = dot(att_ref[...], proj_ref[...])
    gi_s[...] = gi_ref[...].astype(F32)
    levels = wx_ref.shape[0]
    half = TOK // 2
    for level in range(levels):
        back = (level + levels - 1) % levels
        k, z = back // WLEV, back % WLEV
        moved = []
        for src, own_in, own_out in ((br_s, wx_ref, base_ref), (gi_s, gx_ref, gbase_ref)):
            starts = [(2 * k + n) * TOK + z * half for n in range(2)]
            rows = jnp.concatenate([src[at : at + half, :] for at in starts], axis=0).astype(BF)
            own_out[level] = (own_in[level].astype(F32) + dot(pown_ref[...], rows, 0, 0)).astype(BF)
            moved.append(rows)
        for where_ref, strip in ((plat_ref, lat_out), (plon_ref, lon_out), (pdiag_ref, diag_out)):
            strip[level] = jnp.concatenate(
                [dot(where_ref[...], rows, 0, 0) for rows in moved], axis=1
            ).astype(BF)


def add_kernel(base_ref, gbase_ref, lat_in, lon_in, diag_in, slat_ref, slon_ref, sdiag_ref, out_ref, gout_ref):
    for level in range(base_ref.shape[0]):
        up = base_ref[level].astype(F32)
        gup = gbase_ref[level].astype(F32)
        for where_ref, strip in ((slat_ref, lat_in), (slon_ref, lon_in), (sdiag_ref, diag_in)):
            both = strip[level]
            up = up + dot(where_ref[...], both[:, :CH])
            gup = gup + dot(where_ref[...], both[:, CH:])
        out_ref[level] = up.astype(BF)
        gout_ref[level] = gup.astype(BF)


def finish_kernel(
    factor, core_ref, mine_ref, other_ref, gqkv_ref, gproj_ref, ggain_ref, gbias_ref, full_s, table_s,
):
    core = core_ref[0]
    half_rows = PAY // 2
    full_s[pl.ds(pl.multiple_of(core * half_rows, half_rows), half_rows), :] = mine_ref[...].astype(F32) * factor
    full_s[pl.ds(pl.multiple_of((1 - core) * half_rows, half_rows), half_rows), :] = other_ref[...].astype(F32) * factor
    tiles = [full_s[j * CH : (j + 1) * CH, :] for j in range(WTILES)]
    for j in range(4):
        gqkv_ref[:, j * LANES : (j + 1) * LANES] = tiles[j]
    cut = 3 * CH - 4 * LANES
    gqkv_ref[:, 4 * LANES :] = tiles[4][:, :cut]
    gproj_ref[...] = jnp.concatenate([tiles[4][:, cut:], tiles[5]], axis=1)
    ggain_ref[...] = jnp.concatenate(
        [full_s[GROW : GROW + 1, :], full_s[GROW + 1 : GROW + 2, : CH - LANES]], axis=1
    )
    pairs = BIAS_ROWS // GROUPS
    levs = pairs // HEADS
    for m in range(GROUPS):
        z_j, a_j = divmod(m, WLAT)
        block = jnp.concatenate(
            [full_s[pl.ds(BROW + j * BIAS_ROWS + m, pairs, stride=GROUPS), :] for j in range(3)], axis=1
        )
        for g in range(GROUPS):
            z_i, a_i = divmod(g, WLAT)
            to = SPAN * (((z_i * WLEV + z_j) * WLAT + a_i) * WLAT + a_j)
            table_s[:, to : to + SPAN] = block[:, g * SPAN : (g + 1) * SPAN]
    for h in range(HEADS):
        for lev in range(levs):
            r = h * levs + lev
            gbias_ref[lev * HEADS + h] = table_s[r : r + 1, : gbias_ref.shape[2]]


def passed(value, lat_step, lon_step):
    lats, highs, zs = lax.axis_size("lat"), lax.axis_size("yhi"), lax.axis_size("z")
    lons = highs * zs
    pairs = [
        (b * lats + a, (b + lon_step) % lons * lats + (a + lat_step) % lats)
        for b in range(lons)
        for a in range(lats)
    ]
    return lax.ppermute(value, ("yhi", "z", "lat"), pairs)


def swapped(value):
    return lax.ppermute(value, "core", [(0, 1), (1, 0)])


def total_over_devices(keep, send, between, last):
    wide = ("ylo", "yhi", "z")
    peers = lax.axis_size("ylo") * lax.axis_size("yhi") * lax.axis_size("z")
    half = (keep.astype(F32) + swapped(send).astype(F32)).astype(BF)
    inputs, fn = between
    half, inputs = lax.optimization_barrier((half, inputs))
    pieces = lax.all_to_all(half, wide, 0, 0, tiled=True)
    keeps, strips = fn(inputs)
    pieces, _ = lax.optimization_barrier((pieces, strips))
    backs = [passed(strip, *step) for strip, step in zip(strips, ((1, 0), (0, 1), (1, 1)))]
    piece = jnp.sum(pieces.reshape(peers, PIECE, LANES).astype(F32), axis=0)
    lats = lax.axis_size("lat")
    place_here = lax.axis_index("core") * peers + lax.axis_index(wide)
    shared = jnp.logical_or(place_here < BROW // PIECE, place_here >= GROW // PIECE)
    others = [
        lax.ppermute(piece, "lat", [(a, (a + step) % lats) for a in range(lats)]) for step in range(1, lats)
    ]
    others, backs = lax.optimization_barrier((others, tuple(backs)))
    others = sum(others)
    piece = jnp.where(shared, piece + others, piece).astype(BF)
    spread = jnp.broadcast_to(piece[None], (peers, PIECE, LANES)).reshape(half.shape)
    spread, backs = lax.optimization_barrier((spread, backs))
    mine = lax.all_to_all(spread, wide, 0, 0, tiled=True)
    mine, outs = lax.optimization_barrier((mine, last(*keeps, *backs)))
    return mine, swapped(mine), outs


def call(kernel, out_shape, scratch=(), smem=0, count=0, flops=0, far=0):
    specs = [pl.BlockSpec(memory_space=pltpu.SMEM)] * smem
    specs += [pl.BlockSpec(memory_space=pltpu.VMEM)] * (count - smem - far)
    specs += [pl.BlockSpec(memory_space=pl.ANY)] * far
    return pl.pallas_call(
        kernel,
        out_shape=out_shape,
        in_specs=specs,
        out_specs=jax.tree.map(lambda _: pl.BlockSpec(memory_space=pltpu.VMEM), out_shape),
        scratch_shapes=list(scratch),
        compiler_params=pltpu.CompilerParams(vmem_limit_bytes=VMEM_LIMIT),
        cost_estimate=pl.CostEstimate(flops=flops, bytes_accessed=flops // 500, transcendentals=0),
    )


def sds(shape, dtype):
    return jax.ShapeDtypeStruct(shape, dtype)


def shards(weather, cotangent, norm_gain, qkv_weight, proj_weight, bias_table):
    samples, levels, rows_here, cols_here, channels = weather.shape
    lat_index = lax.axis_index("lat")
    lat_count = lax.axis_size("lat")
    plane = rows_here * cols_here
    own_cols = cols_here - SHIFT_LON
    wx = weather.reshape(levels, plane, CH)
    gx = cotangent.reshape(levels, plane, CH)
    edge = SHIFT_LAT * SHIFT_LON
    lat_shape = sds((levels, SHIFT_LAT * own_cols, 2 * CH), BF)
    edge_shape = sds((levels, edge, 2 * CH), BF)
    slat, scor = scatter_matrices(cols_here)
    scatter = (slat, scor[:, :edge], scor[:, edge:])
    strips = call(prep_kernel, (lat_shape, edge_shape, edge_shape), count=5, flops=10**9)(
        wx, gx, *[jnp.asarray(m.T, BF) for m in scatter]
    )
    lat_in = passed(strips[0], -1, 0)
    lon_in = passed(strips[1], 0, -1)
    diag_in = passed(strips[2], -1, -1)

    lev_windows = bias_table.shape[0]
    pairs = lev_windows * HEADS
    entries = bias_table.shape[-1]
    table = bias_table.transpose(0, 2, 1, 3).reshape(pairs, 1, entries)
    last = (lat_index == lat_count - 1).astype(jnp.int32).reshape(1)
    sel = jnp.asarray(lon_selectors(), BF)
    bias_rows = lev_windows * TOK
    flat_shape = pltpu.VMEM((pairs, -(-entries // LANES) * LANES), F32)
    bias_shape = (HTILES, bias_rows, LANES)
    bias = call(
        expand_kernel,
        sds(bias_shape, F32),
        scratch=[flat_shape, pltpu.VMEM((GROUPS, pairs, 3 * LANES), F32), pltpu.VMEM((3, BIAS_ROWS, LANES), F32)],
        smem=1, count=3, flops=10**9,
    )(last, table, sel)

    own_m, lat_m, corner_m = gather_matrices(cols_here)
    mats = [jnp.asarray(m, BF) for m in (own_m, lat_m, corner_m[:, :edge], corner_m[:, edge:])]
    wqkv = qkv_weight.reshape(CH, 3, CH).transpose(1, 0, 2)
    tokens = levels * plane
    plane_shape = sds((levels, plane, CH), BF)
    token_shape = sds((tokens, CH), BF)
    core = lax.axis_index("core").astype(jnp.int32).reshape(1)
    half_shape = sds((PAY // 2, LANES), BF)
    wide_f = pltpu.VMEM((tokens, CH), F32)
    wide_b = pltpu.VMEM((tokens, CH), BF)
    att, gi, keep, send = call(
        main_kernel,
        (token_shape, token_shape, half_shape, half_shape),
        scratch=[wide_f, wide_f, wide_f, pltpu.VMEM((tokens, LANES), F32)]
        + [wide_b] * 7
        + [
            pltpu.VMEM((CH, tokens), BF),
            pltpu.VMEM(bias_shape, F32),
            pltpu.VMEM((PAY, LANES), F32),
            pltpu.VMEM(bias_shape, F32),
            pltpu.VMEM(sel.shape, BF),
            pltpu.SemaphoreType.DMA((2,)),
        ],
        smem=1,
        count=15,
        far=2,
        flops=10**10,
    )(core, wx, gx, lat_in, lon_in, diag_in, norm_gain.reshape(1, CH), wqkv, proj_weight, *mats, bias, sel)

    def give_back(inputs):
        base, gbase, *strips = call(
            return_kernel,
            (plane_shape, plane_shape, lat_shape, edge_shape, edge_shape),
            scratch=[wide_f, wide_f],
            count=9,
            flops=2 * 10**9,
        )(wx, gx, *inputs, proj_weight, *mats)
        return (base, gbase), strips

    def add_up(*parts):
        return call(add_kernel, (plane_shape, plane_shape), count=8, flops=2 * 10**9)(
            *parts, *[jnp.asarray(m, BF) for m in scatter]
        )

    mine, other, (out, gout) = total_over_devices(keep, send, ((att, gi), give_back), add_up)
    factor = (samples * levels * rows_here * cols_here * lax.axis_size(("ylo", "core", "yhi", "z", "lat"))) ** (-0.5)
    gqkv, gproj, ggain, gbias = call(
        functools.partial(finish_kernel, factor),
        (sds(qkv_weight.shape, F32), sds(proj_weight.shape, F32), sds((1, CH), F32), sds((pairs, 1, entries), F32)),
        scratch=[pltpu.VMEM((PAY, LANES), F32), flat_shape],
        smem=1,
        count=3,
        flops=10**9,
    )(core, mine, other)
    return (
        out.reshape(weather.shape),
        gout.reshape(weather.shape),
        gqkv,
        gproj,
        ggain.reshape(CH),
        gbias.reshape(lev_windows, HEADS, 1, entries).transpose(0, 2, 1, 3),
    )


def solution(mesh):
    fine = jax.sharding.Mesh(mesh.devices.reshape(2, 2, 2, 8, 4), ("ylo", "core", "yhi", "z", "lat"))
    dp, lon = ("ylo", "core"), ("yhi", "z")
    grid = P(dp, None, "lat", lon, None)
    table = P(None, "lat", None, None)
    return jax.shard_map(
        shards,
        mesh=fine,
        in_specs=(grid, grid, P(), P(), P(), table),
        out_specs=(grid, grid, P(), P(), P(), table),
        check_vma=False,
    )
```

```python
import functools

import numpy as np
import jax
import jax.numpy as jnp
from jax import lax
from jax.experimental import pallas as pl
from jax.experimental.pallas import tpu as pltpu
from jax.sharding import PartitionSpec as P

HEADS = 6
WLEV = 2
WLAT = 6
WLON = 12
HD = 32
CH = 192
TOK = 144
LANES = 128
SHIFT_LAT = 3
SHIFT_LON = 6
SPAN = 2 * WLON - 1
GROUPS = WLEV * WLAT
MASKED = -1e30
EPSILON = 1e-05
BF = jnp.bfloat16
F32 = jnp.float32
PAY = 2048
WTILES = 6
BIAS_ROWS = 288
BROW = WTILES * CH
GROW = BROW + 3 * BIAS_ROWS
PIECE = 32
HTILES = 7
HLANES = HTILES * LANES
CHUNK = 3 * LANES
MIB = 1024 * 1024


def one_hot(rows, cols, choose):
    row = lax.broadcasted_iota(jnp.int32, (rows, cols), 0)
    col = lax.broadcasted_iota(jnp.int32, (rows, cols), 1)
    return jnp.where(choose(row) == col, 1.0, 0.0).astype(BF)


def window_places(cols_here):
    own_cols = cols_here - SHIFT_LON
    plane = WLAT * cols_here
    strip = SHIFT_LAT * SHIFT_LON

    def chooser(low_rows, low_cols, first, stride, offset):
        def choose(row):
            a = row // WLON % WLAT
            col = row // (WLAT * WLON) * WLON + row % WLON
            inside_rows = a < SHIFT_LAT if low_rows else a >= SHIFT_LAT
            inside_cols = col < own_cols if low_cols else col >= own_cols
            source = (a + first) * stride + col + offset
            return jnp.where(jnp.logical_and(inside_rows, inside_cols), source, -1)

        return choose

    return (
        one_hot(plane, plane, chooser(True, True, SHIFT_LAT, cols_here, SHIFT_LON)),
        one_hot(plane, SHIFT_LAT * own_cols, chooser(False, True, -SHIFT_LAT, own_cols, 0)),
        one_hot(plane, strip, chooser(True, False, 0, SHIFT_LON, -own_cols)),
        one_hot(plane, strip, chooser(False, False, -SHIFT_LAT, SHIFT_LON, -own_cols)),
    )


def strip_places(cols_here):
    own_cols = cols_here - SHIFT_LON
    plane = WLAT * cols_here
    strip = SHIFT_LAT * SHIFT_LON
    return (
        one_hot(SHIFT_LAT * own_cols, plane, lambda i: i // own_cols * cols_here + SHIFT_LON + i % own_cols),
        one_hot(strip, plane, lambda i: (i // SHIFT_LON + SHIFT_LAT) * cols_here + i % SHIFT_LON),
        one_hot(strip, plane, lambda i: i // SHIFT_LON * cols_here + i % SHIFT_LON),
    )


def lon_selectors():
    out = np.zeros((WLON, 3 * LANES, 2 * LANES), np.float32)
    for xj in range(WLON):
        for g in range(GROUPS):
            for xi in range(WLON):
                out[xj, g * SPAN + xi - xj + WLON - 1, g * WLON + xi] = 1
    return out


def dot(a, b, ca=1, cb=0):
    return lax.dot_general(a, b, (((ca,), (cb,)), ((), ())), preferred_element_type=F32)


def split(value):
    high = value.astype(BF)
    return high, (value - high.astype(F32)).astype(BF)


def prep_kernel(wx_far, gx_far, lat_out, lon_out, diag_out, wx_ref, gx_ref, sems):
    copies = [
        pltpu.make_async_copy(far, near, sems.at[i]) for i, (far, near) in enumerate(((wx_far, wx_ref), (gx_far, gx_ref)))
    ]
    for copy in copies:
        copy.start()
    picks = strip_places(wx_ref.shape[1] // WLAT)
    for copy in copies:
        copy.wait()
    for level in range(wx_ref.shape[0]):
        for pick, strip in zip(picks, (lat_out, lon_out, diag_out)):
            strip[level] = jnp.concatenate([dot(pick, ref[level]) for ref in (wx_ref, gx_ref)], axis=1).astype(BF)


def expand_kernel(last_ref, table_ref, sel_ref, bias_ref, flat_s, block_s, table_s):
    pairs, _, entries = table_ref.shape
    levs = pairs // HEADS
    for h in range(HEADS):
        for lev in range(levs):
            r = h * levs + lev
            flat_s[r : r + 1, :entries] = table_ref[lev * HEADS + h]
    for m in range(GROUPS):
        z_j, a_j = divmod(m, WLAT)
        for g in range(GROUPS):
            z_i, a_i = divmod(g, WLAT)
            at = SPAN * (((z_i * WLEV + z_j) * WLAT + a_i) * WLAT + a_j)
            block_s[m, :, g * SPAN : (g + 1) * SPAN] = flat_s[:, at : at + SPAN]
        for j in range(3):
            table_s[j, pl.ds(m, pairs, stride=GROUPS), :] = block_s[m, :, j * LANES : (j + 1) * LANES]
    table = jnp.concatenate([table_s[j] for j in range(3)], axis=1)[:, : GROUPS * SPAN]
    high, low = split(table)
    rows = levs * GROUPS
    row_id = lax.broadcasted_iota(jnp.int32, (BIAS_ROWS, TOK), 0)
    col_id = lax.broadcasted_iota(jnp.int32, (BIAS_ROWS, TOK), 1)
    m_j = row_id % GROUPS
    lev = row_id // GROUPS % levs
    a_i = col_id // WLON % WLAT
    z_i = col_id // (WLON * WLAT)
    cross_lev = jnp.logical_and(lev == levs - 1, m_j // WLAT != z_i)
    cross_lat = jnp.logical_and(last_ref[0] == 1, (m_j % WLAT >= SHIFT_LAT) != (a_i >= SHIFT_LAT))
    hide = jnp.where(jnp.logical_or(cross_lev, cross_lat), MASKED, 0.0)
    pad = jnp.zeros((rows, HLANES - HEADS * TOK), F32)
    for xj in range(WLON):
        sel = sel_ref[xj, : GROUPS * SPAN, :TOK]
        value = dot(high, sel) + dot(low, sel) + hide
        wide = jnp.concatenate([value[h * rows : (h + 1) * rows] for h in range(HEADS)] + [pad], axis=1)
        for t in range(HTILES):
            bias_ref[t, pl.ds(xj, rows, stride=WLON), :] = wide[:, t * LANES : (t + 1) * LANES]


def main_kernel(
    core_ref, wx_ref, gx_ref, lat_in, lon_in, diag_in, gain_ref, wqkv_ref, proj_ref,
    bias_hbm, sel_hbm,
    att_ref, gi_ref, keep_ref, send_ref,
    x_s, g_s, normed_s, inv_s, q_s, k_s, v_s, da_s, dq_s, dk_s, dv_s, hid_t, dsum_s, pay_s, bias_s, sel_s, sems,
):
    bias_copy = pltpu.make_async_copy(bias_hbm, bias_s, sems.at[0])
    sel_copy = pltpu.make_async_copy(sel_hbm, sel_s, sems.at[1])
    bias_copy.start()
    sel_copy.start()
    levels = wx_ref.shape[0]
    half = TOK // 2
    windows = x_s.shape[0] // TOK
    place_own, *places = window_places(wx_ref.shape[1] // WLAT)
    for level in range(levels):
        back = (level + levels - 1) % levels
        k, z = back // WLEV, back % WLEV
        xw = dot(place_own, wx_ref[level])
        gw = dot(place_own, gx_ref[level])
        for place, strip in zip(places, (lat_in, lon_in, diag_in)):
            both = strip[level]
            xw = xw + dot(place, both[:, :CH])
            gw = gw + dot(place, both[:, CH:])
        for n in range(2):
            at = (2 * k + n) * TOK + z * half
            x_s[at : at + half, :] = xw[n * half : (n + 1) * half]
            g_s[at : at + half, :] = gw[n * half : (n + 1) * half]

    gain = gain_ref[...]
    inv_root = HD ** (-0.5)

    def eye(n):
        return (lax.broadcasted_iota(jnp.int32, (n, n), 0) == lax.broadcasted_iota(jnp.int32, (n, n), 1)).astype(F32).astype(BF)

    eye_c = eye(CH)
    eye_t = eye(TOK)
    chunks = [slice(at, at + CHUNK) for at in range(0, x_s.shape[0], CHUNK)]
    for rows in chunks:
        x = x_s[rows]
        centred = x - jnp.mean(x, axis=-1, keepdims=True)
        inv_std = lax.rsqrt(jnp.mean(centred * centred, axis=-1, keepdims=True) + EPSILON)
        normed = centred * inv_std
        normed_s[rows] = normed
        inv_s[rows] = jnp.broadcast_to(inv_std, (CHUNK, LANES))
        hidden = (normed * gain).astype(BF)
        q_s[rows] = (dot(hidden, wqkv_ref[0]) * inv_root).astype(BF)
        k_s[rows] = dot(hidden, wqkv_ref[1]).astype(BF)
        v_s[rows] = dot(hidden, wqkv_ref[2]).astype(BF)
        da_s[rows] = dot(g_s[rows].astype(BF), proj_ref[...], 1, 1).astype(BF)
        hid_t[:, rows] = dot(eye_c, hidden, 1, 1).astype(BF)

    channel = lax.broadcasted_iota(jnp.int32, (TOK, CH), 1)
    head_mask = [jnp.logical_and(channel >= h * HD, channel < (h + 1) * HD) for h in range(HEADS)]
    zero = jnp.zeros((TOK, CH), BF)
    tail = jnp.zeros((HLANES - HEADS * TOK, CH), BF)

    def per_head(value):
        return jnp.concatenate([jnp.where(mask, value, zero) for mask in head_mask] + [tail], axis=0)

    bias_copy.wait()
    gproj = jnp.zeros((CH, CH), F32)
    for w in range(windows):
        rows = slice(w * TOK, (w + 1) * TOK)
        first = w % 2 == 0
        lev_rows = slice(w // 2 * TOK, (w // 2 + 1) * TOK)
        key, v = k_s[rows], v_s[rows]
        q_heads = per_head(q_s[rows])
        da_heads = per_head(da_s[rows])
        key_t = dot(eye_c, key, 1, 1).astype(BF)
        v_t = dot(eye_c, v, 1, 1).astype(BF)
        scores = dot(key, q_heads, 1, 1)
        scores = scores + jnp.concatenate([bias_s[t, lev_rows, :] for t in range(HTILES)], axis=1)
        dp = dot(v, da_heads, 1, 1)
        e = jnp.exp(scores - jnp.max(scores, axis=0, keepdims=True))
        probs = (e * (1.0 / jnp.sum(e, axis=0, keepdims=True))).astype(BF)
        dv_s[rows] = dot(probs, da_heads).astype(BF)
        pf = probs.astype(F32)
        t_prod = pf * dp
        ds = t_prod - pf * jnp.sum(t_prod, axis=0, keepdims=True)
        dsb = ds.astype(BF)
        for t in range(HTILES):
            part = ds[:, t * LANES : (t + 1) * LANES]
            dsum_s[t, lev_rows, :] = part if first else dsum_s[t, lev_rows, :] + part
        dk_s[rows] = dot(dsb, q_heads).astype(BF)
        att_t = jnp.concatenate(
            [dot(v_t[h * HD : (h + 1) * HD], probs[:, h * TOK : (h + 1) * TOK]) for h in range(HEADS)], axis=0
        ).astype(BF)
        dq_t = jnp.concatenate(
            [dot(key_t[h * HD : (h + 1) * HD], dsb[:, h * TOK : (h + 1) * TOK]) for h in range(HEADS)], axis=0
        )
        dq_t = (dq_t * inv_root).astype(BF)
        att_ref[rows] = dot(eye_t, att_t, 1, 1).astype(BF)
        dq_s[rows] = dot(eye_t, dq_t, 1, 1).astype(BF)
        gproj = gproj + dot(att_t, g_s[rows].astype(BF))

    g_gain = jnp.zeros((1, CH), F32)
    for rows in chunks:
        gh = (
            dot(dq_s[rows], wqkv_ref[0], 1, 1)
            + dot(dk_s[rows], wqkv_ref[1], 1, 1)
            + dot(dv_s[rows], wqkv_ref[2], 1, 1)
        )
        normed = normed_s[rows]
        g_gain = g_gain + jnp.sum(gh * normed, axis=0, keepdims=True)
        gn = gh * gain
        gi = inv_s[rows][:, :1] * (
            gn
            - jnp.mean(gn, axis=-1, keepdims=True)
            - normed * jnp.mean(gn * normed, axis=-1, keepdims=True)
        )
        gi_ref[rows] = gi.astype(BF)

    g_wide = [dot(hid_t[...], part[...]) for part in (dq_s, dk_s, dv_s)]
    weights = jnp.concatenate(g_wide + [gproj], axis=1)
    for j in range(WTILES):
        pay_s[j * CH : (j + 1) * CH, :] = weights[:, j * LANES : (j + 1) * LANES]
    pay_s[GROW:, :] = jnp.zeros((PAY - GROW, LANES), F32)
    pay_s[GROW : GROW + 1, :] = g_gain[:, :LANES]
    pay_s[GROW + 1 : GROW + 2, : CH - LANES] = g_gain[:, LANES:]

    sel_copy.wait()
    lev_groups = dsum_s.shape[1] // WLON
    g_bias = jnp.zeros((BIAS_ROWS, 3 * LANES), F32)
    for xj in range(WLON):
        wide = jnp.concatenate(
            [dsum_s[t, pl.ds(xj, lev_groups, stride=WLON), :] for t in range(HTILES)], axis=1
        ).astype(BF)
        stacked = jnp.concatenate([wide[:, h * TOK : (h + 1) * TOK] for h in range(HEADS)], axis=0)
        g_bias = g_bias + dot(stacked, sel_s[xj, :, :TOK], 1, 1)
    for j in range(3):
        pay_s[BROW + j * BIAS_ROWS : BROW + (j + 1) * BIAS_ROWS, :] = g_bias[:, j * LANES : (j + 1) * LANES]
    core = core_ref[0]
    half_rows = PAY // 2
    keep_ref[...] = pay_s[pl.ds(pl.multiple_of(core * half_rows, half_rows), half_rows), :].astype(BF)
    send_ref[...] = pay_s[pl.ds(pl.multiple_of((1 - core) * half_rows, half_rows), half_rows), :].astype(BF)


def return_kernel(
    wx_ref, gx_ref, att_ref, gi_ref, proj_ref,
    base_ref, gbase_ref, lat_out, lon_out, diag_out, br_s, gi_s,
):
    br_s[...] = dot(att_ref[...], proj_ref[...])
    gi_s[...] = gi_ref[...].astype(F32)
    place_own, *places = window_places(wx_ref.shape[1] // WLAT)
    levels = wx_ref.shape[0]
    half = TOK // 2
    for level in range(levels):
        back = (level + levels - 1) % levels
        k, z = back // WLEV, back % WLEV
        moved = []
        for src, own_in, own_out in ((br_s, wx_ref, base_ref), (gi_s, gx_ref, gbase_ref)):
            starts = [(2 * k + n) * TOK + z * half for n in range(2)]
            rows = jnp.concatenate([src[at : at + half, :] for at in starts], axis=0).astype(BF)
            own_out[level] = (own_in[level].astype(F32) + dot(place_own, rows, 0, 0)).astype(BF)
            moved.append(rows)
        for place, strip in zip(places, (lat_out, lon_out, diag_out)):
            strip[level] = jnp.concatenate(
                [dot(place, rows, 0, 0) for rows in moved], axis=1
            ).astype(BF)


def add_kernel(base_ref, gbase_ref, lat_in, lon_in, diag_in, out_ref, gout_ref):
    picks = strip_places(base_ref.shape[1] // WLAT)
    for level in range(base_ref.shape[0]):
        up = base_ref[level].astype(F32)
        gup = gbase_ref[level].astype(F32)
        for pick, strip in zip(picks, (lat_in, lon_in, diag_in)):
            both = strip[level]
            up = up + dot(pick, both[:, :CH], 0, 0)
            gup = gup + dot(pick, both[:, CH:], 0, 0)
        out_ref[level] = up.astype(BF)
        gout_ref[level] = gup.astype(BF)


def finish_kernel(
    factor, core_ref, mine_ref, other_ref, gqkv_ref, gproj_ref, ggain_ref, gbias_ref, full_s, table_s,
):
    core = core_ref[0]
    half_rows = PAY // 2
    full_s[pl.ds(pl.multiple_of(core * half_rows, half_rows), half_rows), :] = mine_ref[...].astype(F32) * factor
    full_s[pl.ds(pl.multiple_of((1 - core) * half_rows, half_rows), half_rows), :] = other_ref[...].astype(F32) * factor
    tiles = [full_s[j * CH : (j + 1) * CH, :] for j in range(WTILES)]
    for j in range(4):
        gqkv_ref[:, j * LANES : (j + 1) * LANES] = tiles[j]
    cut = 3 * CH - 4 * LANES
    gqkv_ref[:, 4 * LANES :] = tiles[4][:, :cut]
    gproj_ref[...] = jnp.concatenate([tiles[4][:, cut:], tiles[5]], axis=1)
    ggain_ref[...] = jnp.concatenate(
        [full_s[GROW : GROW + 1, :], full_s[GROW + 1 : GROW + 2, : CH - LANES]], axis=1
    )
    pairs = BIAS_ROWS // GROUPS
    levs = pairs // HEADS
    for m in range(GROUPS):
        z_j, a_j = divmod(m, WLAT)
        block = jnp.concatenate(
            [full_s[pl.ds(BROW + j * BIAS_ROWS + m, pairs, stride=GROUPS), :] for j in range(3)], axis=1
        )
        for g in range(GROUPS):
            z_i, a_i = divmod(g, WLAT)
            to = SPAN * (((z_i * WLEV + z_j) * WLAT + a_i) * WLAT + a_j)
            table_s[:, to : to + SPAN] = block[:, g * SPAN : (g + 1) * SPAN]
    for h in range(HEADS):
        for lev in range(levs):
            r = h * levs + lev
            gbias_ref[lev * HEADS + h] = table_s[r : r + 1, : gbias_ref.shape[2]]


def passed(value, lat_step, lon_step):
    lats, highs, zs = lax.axis_size("lat"), lax.axis_size("yhi"), lax.axis_size("z")
    lons = highs * zs
    pairs = [
        (b * lats + a, (b + lon_step) % lons * lats + (a + lat_step) % lats)
        for b in range(lons)
        for a in range(lats)
    ]
    return lax.ppermute(value, ("yhi", "z", "lat"), pairs)


def swapped(value):
    return lax.ppermute(value, "core", [(0, 1), (1, 0)])


def total_over_devices(keep, send, between, last):
    wide = ("ylo", "yhi", "z")
    peers = lax.axis_size("ylo") * lax.axis_size("yhi") * lax.axis_size("z")
    half = (keep.astype(F32) + swapped(send).astype(F32)).astype(BF)
    inputs, fn = between
    half, inputs = lax.optimization_barrier((half, inputs))
    pieces = lax.all_to_all(half, wide, 0, 0, tiled=True)
    keeps, strips = fn(inputs)
    pieces, _ = lax.optimization_barrier((pieces, strips))
    backs = [passed(strip, *step) for strip, step in zip(strips, ((1, 0), (0, 1), (1, 1)))]
    piece = jnp.sum(pieces.reshape(peers, PIECE, LANES).astype(F32), axis=0)
    lats = lax.axis_size("lat")
    place_here = lax.axis_index("core") * peers + lax.axis_index(wide)
    shared = jnp.logical_or(place_here < BROW // PIECE, place_here >= GROW // PIECE)
    others = [
        lax.ppermute(piece, "lat", [(a, (a + step) % lats) for a in range(lats)]) for step in range(1, lats)
    ]
    others, backs = lax.optimization_barrier((others, tuple(backs)))
    others = sum(others)
    piece = jnp.where(shared, piece + others, piece).astype(BF)
    spread = jnp.broadcast_to(piece[None], (peers, PIECE, LANES)).reshape(half.shape)
    spread, backs = lax.optimization_barrier((spread, backs))
    mine = lax.all_to_all(spread, wide, 0, 0, tiled=True)
    mine, outs = lax.optimization_barrier((mine, last(*keeps, *backs)))
    return mine, swapped(mine), outs


def call(kernel, out_shape, scratch=(), smem=0, count=0, flops=0, far=0, room=12):
    specs = [pl.BlockSpec(memory_space=pltpu.SMEM)] * smem
    specs += [pl.BlockSpec(memory_space=pltpu.VMEM)] * (count - smem - far)
    specs += [pl.BlockSpec(memory_space=pl.ANY)] * far
    return pl.pallas_call(
        kernel,
        out_shape=out_shape,
        in_specs=specs,
        out_specs=jax.tree.map(lambda _: pl.BlockSpec(memory_space=pltpu.VMEM), out_shape),
        scratch_shapes=list(scratch),
        compiler_params=pltpu.CompilerParams(vmem_limit_bytes=room * MIB),
        cost_estimate=pl.CostEstimate(flops=flops, bytes_accessed=flops // 500, transcendentals=0),
    )


def sds(shape, dtype):
    return jax.ShapeDtypeStruct(shape, dtype)


def shards(weather, cotangent, norm_gain, qkv_weight, proj_weight, bias_table):
    samples, levels, rows_here, cols_here, channels = weather.shape
    lat_index = lax.axis_index("lat")
    lat_count = lax.axis_size("lat")
    plane = rows_here * cols_here
    own_cols = cols_here - SHIFT_LON
    wx = weather.reshape(levels, plane, CH)
    gx = cotangent.reshape(levels, plane, CH)
    edge = SHIFT_LAT * SHIFT_LON
    lat_shape = sds((levels, SHIFT_LAT * own_cols, 2 * CH), BF)
    edge_shape = sds((levels, edge, 2 * CH), BF)
    near = [pltpu.VMEM((levels, plane, CH), BF)] * 2
    strips = call(
        prep_kernel, (lat_shape, edge_shape, edge_shape), scratch=near + [pltpu.SemaphoreType.DMA((2,))],
        count=2, far=2, flops=10**9,
    )(*[pltpu.with_memory_space_constraint(v, pltpu.HBM) for v in (wx, gx)])
    lat_in = passed(strips[0], -1, 0)
    lon_in = passed(strips[1], 0, -1)
    diag_in = passed(strips[2], -1, -1)

    lev_windows = bias_table.shape[0]
    pairs = lev_windows * HEADS
    entries = bias_table.shape[-1]
    table = bias_table.transpose(0, 2, 1, 3).reshape(pairs, 1, entries)
    last = (lat_index == lat_count - 1).astype(jnp.int32).reshape(1)
    sel = jnp.asarray(lon_selectors(), BF)
    bias_rows = lev_windows * TOK
    flat_shape = pltpu.VMEM((pairs, -(-entries // LANES) * LANES), F32)
    bias_shape = (HTILES, bias_rows, LANES)
    bias = call(
        expand_kernel,
        sds(bias_shape, F32),
        scratch=[flat_shape, pltpu.VMEM((GROUPS, pairs, 3 * LANES), F32), pltpu.VMEM((3, BIAS_ROWS, LANES), F32)],
        smem=1, count=3, flops=10**9,
    )(last, table, sel)

    wqkv = qkv_weight.reshape(CH, 3, CH).transpose(1, 0, 2)
    tokens = levels * plane
    plane_shape = sds((levels, plane, CH), BF)
    token_shape = sds((tokens, CH), BF)
    core = lax.axis_index("core").astype(jnp.int32).reshape(1)
    half_shape = sds((PAY // 2, LANES), BF)
    wide_f = pltpu.VMEM((tokens, CH), F32)
    wide_b = pltpu.VMEM((tokens, CH), BF)
    att, gi, keep, send = call(
        main_kernel,
        (token_shape, token_shape, half_shape, half_shape),
        scratch=[wide_f, wide_f, wide_f, pltpu.VMEM((tokens, LANES), F32)]
        + [wide_b] * 7
        + [
            pltpu.VMEM((CH, tokens), BF),
            pltpu.VMEM(bias_shape, F32),
            pltpu.VMEM((PAY, LANES), F32),
            pltpu.VMEM(bias_shape, F32),
            pltpu.VMEM(sel.shape, BF),
            pltpu.SemaphoreType.DMA((2,)),
        ],
        smem=1,
        count=11,
        far=2,
        flops=10**10,
        room=28,
    )(core, wx, gx, lat_in, lon_in, diag_in, norm_gain.reshape(1, CH), wqkv, proj_weight, bias, sel)

    def give_back(inputs):
        base, gbase, *strips = call(
            return_kernel,
            (plane_shape, plane_shape, lat_shape, edge_shape, edge_shape),
            scratch=[wide_f, wide_f],
            count=5,
            flops=2 * 10**9,
            room=56,
        )(wx, gx, *inputs, proj_weight)
        return (base, gbase), strips

    def add_up(*parts):
        return call(add_kernel, (plane_shape, plane_shape), count=5, flops=2 * 10**9)(*parts)

    mine, other, (out, gout) = total_over_devices(keep, send, ((att, gi), give_back), add_up)
    factor = (samples * levels * rows_here * cols_here * lax.axis_size(("ylo", "core", "yhi", "z", "lat"))) ** (-0.5)
    gqkv, gproj, ggain, gbias = call(
        functools.partial(finish_kernel, factor),
        (sds(qkv_weight.shape, F32), sds(proj_weight.shape, F32), sds((1, CH), F32), sds((pairs, 1, entries), F32)),
        scratch=[pltpu.VMEM((PAY, LANES), F32), flat_shape],
        smem=1,
        count=3,
        flops=10**9,
    )(core, mine, other)
    return (
        out.reshape(weather.shape),
        gout.reshape(weather.shape),
        gqkv,
        gproj,
        ggain.reshape(CH),
        gbias.reshape(lev_windows, HEADS, 1, entries).transpose(0, 2, 1, 3),
    )


def solution(mesh):
    fine = jax.sharding.Mesh(mesh.devices.reshape(2, 2, 2, 8, 4), ("ylo", "core", "yhi", "z", "lat"))
    dp, lon = ("ylo", "core"), ("yhi", "z")
    grid = P(dp, None, "lat", lon, None)
    table = P(None, "lat", None, None)
    return jax.shard_map(
        shards,
        mesh=fine,
        in_specs=(grid, grid, P(), P(), P(), table),
        out_specs=(grid, grid, P(), P(), P(), table),
        check_vma=False,
    )
```

```python
import functools

import numpy as np
import jax
import jax.numpy as jnp
from jax import lax
from jax.experimental import pallas as pl
from jax.experimental.pallas import tpu as pltpu
from jax.sharding import PartitionSpec as P

HEADS = 6
WLEV = 2
WLAT = 6
WLON = 12
HD = 32
CH = 192
TOK = 144
LANES = 128
SHIFT_LAT = 3
SHIFT_LON = 6
SPAN = 2 * WLON - 1
GROUPS = WLEV * WLAT
MASKED = -1e30
EPSILON = 1e-05
BF = jnp.bfloat16
F32 = jnp.float32
PAY = 2048
WTILES = 6
BIAS_ROWS = 288
BROW = WTILES * CH
GROW = BROW + 3 * BIAS_ROWS
PIECE = 32
HTILES = 7
HLANES = HTILES * LANES
CHUNK = 3 * LANES
MIB = 1024 * 1024


def one_hot(rows, cols, choose):
    row = lax.broadcasted_iota(jnp.int32, (rows, cols), 0)
    col = lax.broadcasted_iota(jnp.int32, (rows, cols), 1)
    return jnp.where(choose(row) == col, 1.0, 0.0).astype(BF)


def window_places(cols_here):
    own_cols = cols_here - SHIFT_LON
    plane = WLAT * cols_here
    strip = SHIFT_LAT * SHIFT_LON

    def chooser(low_rows, low_cols, first, stride, offset):
        def choose(row):
            a = row // WLON % WLAT
            col = row // (WLAT * WLON) * WLON + row % WLON
            inside_rows = a < SHIFT_LAT if low_rows else a >= SHIFT_LAT
            inside_cols = col < own_cols if low_cols else col >= own_cols
            source = (a + first) * stride + col + offset
            return jnp.where(jnp.logical_and(inside_rows, inside_cols), source, -1)

        return choose

    return (
        one_hot(plane, plane, chooser(True, True, SHIFT_LAT, cols_here, SHIFT_LON)),
        one_hot(plane, SHIFT_LAT * own_cols, chooser(False, True, -SHIFT_LAT, own_cols, 0)),
        one_hot(plane, strip, chooser(True, False, 0, SHIFT_LON, -own_cols)),
        one_hot(plane, strip, chooser(False, False, -SHIFT_LAT, SHIFT_LON, -own_cols)),
    )


def strip_places(cols_here):
    own_cols = cols_here - SHIFT_LON
    plane = WLAT * cols_here
    strip = SHIFT_LAT * SHIFT_LON
    return (
        one_hot(SHIFT_LAT * own_cols, plane, lambda i: i // own_cols * cols_here + SHIFT_LON + i % own_cols),
        one_hot(strip, plane, lambda i: (i // SHIFT_LON + SHIFT_LAT) * cols_here + i % SHIFT_LON),
        one_hot(strip, plane, lambda i: i // SHIFT_LON * cols_here + i % SHIFT_LON),
    )


def lon_selectors():
    out = np.zeros((WLON, 3 * LANES, 2 * LANES), np.float32)
    for xj in range(WLON):
        for g in range(GROUPS):
            for xi in range(WLON):
                out[xj, g * SPAN + xi - xj + WLON - 1, g * WLON + xi] = 1
    return out


def dot(a, b, ca=1, cb=0):
    return lax.dot_general(a, b, (((ca,), (cb,)), ((), ())), preferred_element_type=F32)


def split(value):
    high = value.astype(BF)
    return high, (value - high.astype(F32)).astype(BF)


def prep_kernel(wx_far, gx_far, lat_out, lon_out, diag_out, wx_ref, gx_ref, sems):
    copies = [
        pltpu.make_async_copy(far, near, sems.at[i]) for i, (far, near) in enumerate(((wx_far, wx_ref), (gx_far, gx_ref)))
    ]
    for copy in copies:
        copy.start()
    picks = strip_places(wx_ref.shape[1] // WLAT)
    for copy in copies:
        copy.wait()
    for level in range(wx_ref.shape[0]):
        for pick, strip in zip(picks, (lat_out, lon_out, diag_out)):
            strip[level] = jnp.concatenate([dot(pick, ref[level]) for ref in (wx_ref, gx_ref)], axis=1).astype(BF)


def expand_kernel(last_ref, table_ref, sel_ref, bias_ref, flat_s, block_s, table_s):
    pairs, _, entries = table_ref.shape
    levs = pairs // HEADS
    for h in range(HEADS):
        for lev in range(levs):
            r = h * levs + lev
            flat_s[r : r + 1, :entries] = table_ref[lev * HEADS + h]
    for m in range(GROUPS):
        z_j, a_j = divmod(m, WLAT)
        for g in range(GROUPS):
            z_i, a_i = divmod(g, WLAT)
            at = SPAN * (((z_i * WLEV + z_j) * WLAT + a_i) * WLAT + a_j)
            block_s[m, :, g * SPAN : (g + 1) * SPAN] = flat_s[:, at : at + SPAN]
        for j in range(3):
            table_s[j, pl.ds(m, pairs, stride=GROUPS), :] = block_s[m, :, j * LANES : (j + 1) * LANES]
    table = jnp.concatenate([table_s[j] for j in range(3)], axis=1)[:, : GROUPS * SPAN]
    high, low = split(table)
    rows = levs * GROUPS
    row_id = lax.broadcasted_iota(jnp.int32, (BIAS_ROWS, TOK), 0)
    col_id = lax.broadcasted_iota(jnp.int32, (BIAS_ROWS, TOK), 1)
    m_j = row_id % GROUPS
    lev = row_id // GROUPS % levs
    a_i = col_id // WLON % WLAT
    z_i = col_id // (WLON * WLAT)
    cross_lev = jnp.logical_and(lev == levs - 1, m_j // WLAT != z_i)
    cross_lat = jnp.logical_and(last_ref[0] == 1, (m_j % WLAT >= SHIFT_LAT) != (a_i >= SHIFT_LAT))
    hide = jnp.where(jnp.logical_or(cross_lev, cross_lat), MASKED, 0.0)
    pad = jnp.zeros((rows, HLANES - HEADS * TOK), F32)
    for xj in range(WLON):
        sel = sel_ref[xj, : GROUPS * SPAN, :TOK]
        value = dot(high, sel) + dot(low, sel) + hide
        wide = jnp.concatenate([value[h * rows : (h + 1) * rows] for h in range(HEADS)] + [pad], axis=1)
        for t in range(HTILES):
            bias_ref[t, pl.ds(xj, rows, stride=WLON), :] = wide[:, t * LANES : (t + 1) * LANES]


def main_kernel(
    core_ref, wx_ref, gx_ref, lat_in, lon_in, diag_in, gain_ref, wqkv_ref, proj_ref,
    bias_hbm, sel_hbm,
    att_far, gi_far, keep_ref, send_ref,
    att_ref, gi_ref, x_s, g_s, normed_s, inv_s, q_s, k_s, v_s, da_s, dq_s, dk_s, dv_s, hid_t, dsum_s, pay_s, bias_s, sel_s, sems,
):
    bias_copy = pltpu.make_async_copy(bias_hbm, bias_s, sems.at[0])
    sel_copy = pltpu.make_async_copy(sel_hbm, sel_s, sems.at[1])
    bias_copy.start()
    sel_copy.start()
    levels = wx_ref.shape[0]
    half = TOK // 2
    windows = x_s.shape[0] // TOK
    place_own, *places = window_places(wx_ref.shape[1] // WLAT)
    for level in range(levels):
        back = (level + levels - 1) % levels
        k, z = back // WLEV, back % WLEV
        xw = dot(place_own, wx_ref[level])
        gw = dot(place_own, gx_ref[level])
        for place, strip in zip(places, (lat_in, lon_in, diag_in)):
            both = strip[level]
            xw = xw + dot(place, both[:, :CH])
            gw = gw + dot(place, both[:, CH:])
        for n in range(2):
            at = (2 * k + n) * TOK + z * half
            x_s[at : at + half, :] = xw[n * half : (n + 1) * half]
            g_s[at : at + half, :] = gw[n * half : (n + 1) * half]

    gain = gain_ref[...]
    inv_root = HD ** (-0.5)

    def eye(n):
        return (lax.broadcasted_iota(jnp.int32, (n, n), 0) == lax.broadcasted_iota(jnp.int32, (n, n), 1)).astype(F32).astype(BF)

    eye_c = eye(CH)
    eye_t = eye(TOK)
    chunks = [slice(at, at + CHUNK) for at in range(0, x_s.shape[0], CHUNK)]
    for rows in chunks:
        x = x_s[rows]
        centred = x - jnp.mean(x, axis=-1, keepdims=True)
        inv_std = lax.rsqrt(jnp.mean(centred * centred, axis=-1, keepdims=True) + EPSILON)
        normed = centred * inv_std
        normed_s[rows] = normed
        inv_s[rows] = jnp.broadcast_to(inv_std, (CHUNK, LANES))
        hidden = (normed * gain).astype(BF)
        q_s[rows] = (dot(hidden, wqkv_ref[0]) * inv_root).astype(BF)
        k_s[rows] = dot(hidden, wqkv_ref[1]).astype(BF)
        v_s[rows] = dot(hidden, wqkv_ref[2]).astype(BF)
        da_s[rows] = dot(g_s[rows].astype(BF), proj_ref[...], 1, 1).astype(BF)
        hid_t[:, rows] = dot(eye_c, hidden, 1, 1).astype(BF)

    channel = lax.broadcasted_iota(jnp.int32, (TOK, CH), 1)
    head_mask = [jnp.logical_and(channel >= h * HD, channel < (h + 1) * HD) for h in range(HEADS)]
    zero = jnp.zeros((TOK, CH), BF)
    tail = jnp.zeros((HLANES - HEADS * TOK, CH), BF)

    def per_head(value):
        return jnp.concatenate([jnp.where(mask, value, zero) for mask in head_mask] + [tail], axis=0)

    bias_copy.wait()
    gproj = jnp.zeros((CH, CH), F32)
    for w in range(windows):
        rows = slice(w * TOK, (w + 1) * TOK)
        first = w % 2 == 0
        lev_rows = slice(w // 2 * TOK, (w // 2 + 1) * TOK)
        key, v = k_s[rows], v_s[rows]
        q_heads = per_head(q_s[rows])
        da_heads = per_head(da_s[rows])
        key_t = dot(eye_c, key, 1, 1).astype(BF)
        v_t = dot(eye_c, v, 1, 1).astype(BF)
        scores = dot(key, q_heads, 1, 1)
        scores = scores + jnp.concatenate([bias_s[t, lev_rows, :] for t in range(HTILES)], axis=1)
        dp = dot(v, da_heads, 1, 1)
        e = jnp.exp(scores - jnp.max(scores, axis=0, keepdims=True))
        probs = (e * (1.0 / jnp.sum(e, axis=0, keepdims=True))).astype(BF)
        dv_s[rows] = dot(probs, da_heads).astype(BF)
        pf = probs.astype(F32)
        t_prod = pf * dp
        ds = t_prod - pf * jnp.sum(t_prod, axis=0, keepdims=True)
        dsb = ds.astype(BF)
        for t in range(HTILES):
            part = ds[:, t * LANES : (t + 1) * LANES]
            dsum_s[t, lev_rows, :] = part if first else dsum_s[t, lev_rows, :] + part
        dk_s[rows] = dot(dsb, q_heads).astype(BF)
        att_t = jnp.concatenate(
            [dot(v_t[h * HD : (h + 1) * HD], probs[:, h * TOK : (h + 1) * TOK]) for h in range(HEADS)], axis=0
        ).astype(BF)
        dq_t = jnp.concatenate(
            [dot(key_t[h * HD : (h + 1) * HD], dsb[:, h * TOK : (h + 1) * TOK]) for h in range(HEADS)], axis=0
        )
        dq_t = (dq_t * inv_root).astype(BF)
        att_ref[rows] = dot(eye_t, att_t, 1, 1).astype(BF)
        dq_s[rows] = dot(eye_t, dq_t, 1, 1).astype(BF)
        gproj = gproj + dot(att_t, g_s[rows].astype(BF))

    att_copy = pltpu.make_async_copy(att_ref, att_far, sems.at[2])
    att_copy.start()
    g_gain = jnp.zeros((1, CH), F32)
    for rows in chunks:
        gh = (
            dot(dq_s[rows], wqkv_ref[0], 1, 1)
            + dot(dk_s[rows], wqkv_ref[1], 1, 1)
            + dot(dv_s[rows], wqkv_ref[2], 1, 1)
        )
        normed = normed_s[rows]
        g_gain = g_gain + jnp.sum(gh * normed, axis=0, keepdims=True)
        gn = gh * gain
        gi = inv_s[rows][:, :1] * (
            gn
            - jnp.mean(gn, axis=-1, keepdims=True)
            - normed * jnp.mean(gn * normed, axis=-1, keepdims=True)
        )
        gi_ref[rows] = gi.astype(BF)

    gi_copy = pltpu.make_async_copy(gi_ref, gi_far, sems.at[3])
    gi_copy.start()
    g_wide = [dot(hid_t[...], part[...]) for part in (dq_s, dk_s, dv_s)]
    weights = jnp.concatenate(g_wide + [gproj], axis=1)
    for j in range(WTILES):
        pay_s[j * CH : (j + 1) * CH, :] = weights[:, j * LANES : (j + 1) * LANES]
    pay_s[GROW:, :] = jnp.zeros((PAY - GROW, LANES), F32)
    pay_s[GROW : GROW + 1, :] = g_gain[:, :LANES]
    pay_s[GROW + 1 : GROW + 2, : CH - LANES] = g_gain[:, LANES:]

    sel_copy.wait()
    lev_groups = dsum_s.shape[1] // WLON
    g_bias = jnp.zeros((BIAS_ROWS, 3 * LANES), F32)
    for xj in range(WLON):
        wide = jnp.concatenate(
            [dsum_s[t, pl.ds(xj, lev_groups, stride=WLON), :] for t in range(HTILES)], axis=1
        ).astype(BF)
        stacked = jnp.concatenate([wide[:, h * TOK : (h + 1) * TOK] for h in range(HEADS)], axis=0)
        g_bias = g_bias + dot(stacked, sel_s[xj, :, :TOK], 1, 1)
    for j in range(3):
        pay_s[BROW + j * BIAS_ROWS : BROW + (j + 1) * BIAS_ROWS, :] = g_bias[:, j * LANES : (j + 1) * LANES]
    core = core_ref[0]
    half_rows = PAY // 2
    keep_ref[...] = pay_s[pl.ds(pl.multiple_of(core * half_rows, half_rows), half_rows), :].astype(BF)
    send_ref[...] = pay_s[pl.ds(pl.multiple_of((1 - core) * half_rows, half_rows), half_rows), :].astype(BF)
    att_copy.wait()
    gi_copy.wait()


def return_kernel(
    wx_ref, gx_ref, att_ref, gi_ref, proj_ref,
    base_ref, gbase_ref, lat_out, lon_out, diag_out, br_s, gi_s,
):
    br_s[...] = dot(att_ref[...], proj_ref[...])
    gi_s[...] = gi_ref[...].astype(F32)
    place_own, *places = window_places(wx_ref.shape[1] // WLAT)
    levels = wx_ref.shape[0]
    half = TOK // 2
    for level in range(levels):
        back = (level + levels - 1) % levels
        k, z = back // WLEV, back % WLEV
        moved = []
        for src, own_in, own_out in ((br_s, wx_ref, base_ref), (gi_s, gx_ref, gbase_ref)):
            starts = [(2 * k + n) * TOK + z * half for n in range(2)]
            rows = jnp.concatenate([src[at : at + half, :] for at in starts], axis=0).astype(BF)
            own_out[level] = (own_in[level].astype(F32) + dot(place_own, rows, 0, 0)).astype(BF)
            moved.append(rows)
        for place, strip in zip(places, (lat_out, lon_out, diag_out)):
            strip[level] = jnp.concatenate(
                [dot(place, rows, 0, 0) for rows in moved], axis=1
            ).astype(BF)


def add_kernel(base_ref, gbase_ref, lat_in, lon_in, diag_in, out_ref, gout_ref):
    picks = strip_places(base_ref.shape[1] // WLAT)
    for level in range(base_ref.shape[0]):
        up = base_ref[level].astype(F32)
        gup = gbase_ref[level].astype(F32)
        for pick, strip in zip(picks, (lat_in, lon_in, diag_in)):
            both = strip[level]
            up = up + dot(pick, both[:, :CH], 0, 0)
            gup = gup + dot(pick, both[:, CH:], 0, 0)
        out_ref[level] = up.astype(BF)
        gout_ref[level] = gup.astype(BF)


def finish_kernel(
    factor, core_ref, mine_ref, other_ref, gqkv_ref, gproj_ref, ggain_ref, gbias_ref, full_s, table_s,
):
    core = core_ref[0]
    half_rows = PAY // 2
    full_s[pl.ds(pl.multiple_of(core * half_rows, half_rows), half_rows), :] = mine_ref[...].astype(F32) * factor
    full_s[pl.ds(pl.multiple_of((1 - core) * half_rows, half_rows), half_rows), :] = other_ref[...].astype(F32) * factor
    tiles = [full_s[j * CH : (j + 1) * CH, :] for j in range(WTILES)]
    for j in range(4):
        gqkv_ref[:, j * LANES : (j + 1) * LANES] = tiles[j]
    cut = 3 * CH - 4 * LANES
    gqkv_ref[:, 4 * LANES :] = tiles[4][:, :cut]
    gproj_ref[...] = jnp.concatenate([tiles[4][:, cut:], tiles[5]], axis=1)
    ggain_ref[...] = jnp.concatenate(
        [full_s[GROW : GROW + 1, :], full_s[GROW + 1 : GROW + 2, : CH - LANES]], axis=1
    )
    pairs = BIAS_ROWS // GROUPS
    levs = pairs // HEADS
    for m in range(GROUPS):
        z_j, a_j = divmod(m, WLAT)
        block = jnp.concatenate(
            [full_s[pl.ds(BROW + j * BIAS_ROWS + m, pairs, stride=GROUPS), :] for j in range(3)], axis=1
        )
        for g in range(GROUPS):
            z_i, a_i = divmod(g, WLAT)
            to = SPAN * (((z_i * WLEV + z_j) * WLAT + a_i) * WLAT + a_j)
            table_s[:, to : to + SPAN] = block[:, g * SPAN : (g + 1) * SPAN]
    for h in range(HEADS):
        for lev in range(levs):
            r = h * levs + lev
            gbias_ref[lev * HEADS + h] = table_s[r : r + 1, : gbias_ref.shape[2]]


def passed(value, lat_step, lon_step):
    lats, highs, zs = lax.axis_size("lat"), lax.axis_size("yhi"), lax.axis_size("z")
    lons = highs * zs
    pairs = [
        (b * lats + a, (b + lon_step) % lons * lats + (a + lat_step) % lats)
        for b in range(lons)
        for a in range(lats)
    ]
    return lax.ppermute(value, ("yhi", "z", "lat"), pairs)


def swapped(value):
    return lax.ppermute(value, "core", [(0, 1), (1, 0)])


def total_over_devices(keep, send, between, last):
    wide = ("ylo", "yhi", "z")
    peers = lax.axis_size("ylo") * lax.axis_size("yhi") * lax.axis_size("z")
    half = (keep.astype(F32) + swapped(send).astype(F32)).astype(BF)
    inputs, fn = between
    half, inputs = lax.optimization_barrier((half, inputs))
    pieces = lax.all_to_all(half, wide, 0, 0, tiled=True)
    keeps, strips = fn(inputs)
    pieces, _ = lax.optimization_barrier((pieces, strips))
    backs = [passed(strip, *step) for strip, step in zip(strips, ((1, 0), (0, 1), (1, 1)))]
    piece = jnp.sum(pieces.reshape(peers, PIECE, LANES).astype(F32), axis=0)
    lats = lax.axis_size("lat")
    place_here = lax.axis_index("core") * peers + lax.axis_index(wide)
    shared = jnp.logical_or(place_here < BROW // PIECE, place_here >= GROW // PIECE)
    others = [
        lax.ppermute(piece, "lat", [(a, (a + step) % lats) for a in range(lats)]) for step in range(1, lats)
    ]
    others, backs = lax.optimization_barrier((others, tuple(backs)))
    others = sum(others)
    piece = jnp.where(shared, piece + others, piece).astype(BF)
    spread = jnp.broadcast_to(piece[None], (peers, PIECE, LANES)).reshape(half.shape)
    spread, backs = lax.optimization_barrier((spread, backs))
    mine = lax.all_to_all(spread, wide, 0, 0, tiled=True)
    mine, outs = lax.optimization_barrier((mine, last(*keeps, *backs)))
    return mine, swapped(mine), outs


def call(kernel, out_shape, scratch=(), smem=0, count=0, flops=0, far=0, room=12, far_out=()):
    specs = [pl.BlockSpec(memory_space=pltpu.SMEM)] * smem
    specs += [pl.BlockSpec(memory_space=pltpu.VMEM)] * (count - smem - far)
    specs += [pl.BlockSpec(memory_space=pl.ANY)] * far
    return pl.pallas_call(
        kernel,
        out_shape=out_shape,
        in_specs=specs,
        out_specs=jax.tree.unflatten(
            jax.tree.structure(out_shape),
            [
                pl.BlockSpec(memory_space=pl.ANY if i in far_out else pltpu.VMEM)
                for i in range(len(jax.tree.leaves(out_shape)))
            ],
        ),
        scratch_shapes=list(scratch),
        compiler_params=pltpu.CompilerParams(vmem_limit_bytes=room * MIB),
        cost_estimate=pl.CostEstimate(flops=flops, bytes_accessed=flops // 500, transcendentals=0),
    )


def sds(shape, dtype):
    return jax.ShapeDtypeStruct(shape, dtype)


def shards(weather, cotangent, norm_gain, qkv_weight, proj_weight, bias_table):
    samples, levels, rows_here, cols_here, channels = weather.shape
    lat_index = lax.axis_index("lat")
    lat_count = lax.axis_size("lat")
    plane = rows_here * cols_here
    own_cols = cols_here - SHIFT_LON
    wx = weather.reshape(levels, plane, CH)
    gx = cotangent.reshape(levels, plane, CH)
    edge = SHIFT_LAT * SHIFT_LON
    lat_shape = sds((levels, SHIFT_LAT * own_cols, 2 * CH), BF)
    edge_shape = sds((levels, edge, 2 * CH), BF)
    near = [pltpu.VMEM((levels, plane, CH), BF)] * 2
    strips = call(
        prep_kernel, (lat_shape, edge_shape, edge_shape), scratch=near + [pltpu.SemaphoreType.DMA((2,))],
        count=2, far=2, flops=10**9,
    )(*[pltpu.with_memory_space_constraint(v, pltpu.HBM) for v in (wx, gx)])
    lat_in = passed(strips[0], -1, 0)
    lon_in = passed(strips[1], 0, -1)
    diag_in = passed(strips[2], -1, -1)

    lev_windows = bias_table.shape[0]
    pairs = lev_windows * HEADS
    entries = bias_table.shape[-1]
    table = bias_table.transpose(0, 2, 1, 3).reshape(pairs, 1, entries)
    last = (lat_index == lat_count - 1).astype(jnp.int32).reshape(1)
    sel = jnp.asarray(lon_selectors(), BF)
    bias_rows = lev_windows * TOK
    flat_shape = pltpu.VMEM((pairs, -(-entries // LANES) * LANES), F32)
    bias_shape = (HTILES, bias_rows, LANES)
    bias = call(
        expand_kernel,
        sds(bias_shape, F32),
        scratch=[flat_shape, pltpu.VMEM((GROUPS, pairs, 3 * LANES), F32), pltpu.VMEM((3, BIAS_ROWS, LANES), F32)],
        smem=1, count=3, flops=10**9,
    )(last, table, sel)

    wqkv = qkv_weight.reshape(CH, 3, CH).transpose(1, 0, 2)
    tokens = levels * plane
    plane_shape = sds((levels, plane, CH), BF)
    token_shape = sds((tokens, CH), BF)
    core = lax.axis_index("core").astype(jnp.int32).reshape(1)
    half_shape = sds((PAY // 2, LANES), BF)
    wide_f = pltpu.VMEM((tokens, CH), F32)
    wide_b = pltpu.VMEM((tokens, CH), BF)
    att, gi, keep, send = call(
        main_kernel,
        (pltpu.HBM(token_shape.shape, BF), pltpu.HBM(token_shape.shape, BF), half_shape, half_shape),
        scratch=[wide_b, wide_b, wide_f, wide_f, wide_f, pltpu.VMEM((tokens, LANES), F32)]
        + [wide_b] * 7
        + [
            pltpu.VMEM((CH, tokens), BF),
            pltpu.VMEM(bias_shape, F32),
            pltpu.VMEM((PAY, LANES), F32),
            pltpu.VMEM(bias_shape, F32),
            pltpu.VMEM(sel.shape, BF),
            pltpu.SemaphoreType.DMA((4,)),
        ],
        smem=1,
        count=11,
        far=2,
        far_out=(0, 1),
        flops=10**10,
        room=28,
    )(core, wx, gx, lat_in, lon_in, diag_in, norm_gain.reshape(1, CH), wqkv, proj_weight, bias, sel)

    def give_back(inputs):
        base, gbase, *strips = call(
            return_kernel,
            (plane_shape, plane_shape, lat_shape, edge_shape, edge_shape),
            scratch=[wide_f, wide_f],
            count=5,
            flops=2 * 10**9,
            room=56,
        )(wx, gx, *inputs, proj_weight)
        return (base, gbase), strips

    def add_up(*parts):
        return call(add_kernel, (plane_shape, plane_shape), count=5, flops=2 * 10**9)(*parts)

    mine, other, (out, gout) = total_over_devices(keep, send, ((att, gi), give_back), add_up)
    factor = (samples * levels * rows_here * cols_here * lax.axis_size(("ylo", "core", "yhi", "z", "lat"))) ** (-0.5)
    gqkv, gproj, ggain, gbias = call(
        functools.partial(finish_kernel, factor),
        (sds(qkv_weight.shape, F32), sds(proj_weight.shape, F32), sds((1, CH), F32), sds((pairs, 1, entries), F32)),
        scratch=[pltpu.VMEM((PAY, LANES), F32), flat_shape],
        smem=1,
        count=3,
        flops=10**9,
    )(core, mine, other)
    return (
        out.reshape(weather.shape),
        gout.reshape(weather.shape),
        gqkv,
        gproj,
        ggain.reshape(CH),
        gbias.reshape(lev_windows, HEADS, 1, entries).transpose(0, 2, 1, 3),
    )


def solution(mesh):
    fine = jax.sharding.Mesh(mesh.devices.reshape(2, 2, 2, 8, 4), ("ylo", "core", "yhi", "z", "lat"))
    dp, lon = ("ylo", "core"), ("yhi", "z")
    grid = P(dp, None, "lat", lon, None)
    table = P(None, "lat", None, None)
    return jax.shard_map(
        shards,
        mesh=fine,
        in_specs=(grid, grid, P(), P(), P(), table),
        out_specs=(grid, grid, P(), P(), P(), table),
        check_vma=False,
    )
```

```python
import functools

import numpy as np
import jax
import jax.numpy as jnp
from jax import lax
from jax.experimental import pallas as pl
from jax.experimental.pallas import tpu as pltpu
from jax.sharding import PartitionSpec as P

HEADS = 6
WLEV = 2
WLAT = 6
WLON = 12
HD = 32
CH = 192
TOK = 144
LANES = 128
SHIFT_LAT = 3
SHIFT_LON = 6
SPAN = 2 * WLON - 1
GROUPS = WLEV * WLAT
MASKED = -1e30
EPSILON = 1e-05
BF = jnp.bfloat16
F32 = jnp.float32
PAY = 2048
WTILES = 6
BIAS_ROWS = 288
BROW = WTILES * CH
GROW = BROW + 3 * BIAS_ROWS
PIECE = 32
SPARE = 16
HTILES = 7
HLANES = HTILES * LANES
CHUNK = 3 * LANES
MIB = 1024 * 1024


def one_hot(rows, cols, choose):
    row = lax.broadcasted_iota(jnp.int32, (rows, cols), 0)
    col = lax.broadcasted_iota(jnp.int32, (rows, cols), 1)
    return jnp.where(choose(row) == col, 1.0, 0.0).astype(BF)


def window_places(cols_here):
    own_cols = cols_here - SHIFT_LON
    plane = WLAT * cols_here
    strip = SHIFT_LAT * SHIFT_LON

    def chooser(low_rows, low_cols, first, stride, offset):
        def choose(row):
            a = row // WLON % WLAT
            col = row // (WLAT * WLON) * WLON + row % WLON
            inside_rows = a < SHIFT_LAT if low_rows else a >= SHIFT_LAT
            inside_cols = col < own_cols if low_cols else col >= own_cols
            source = (a + first) * stride + col + offset
            return jnp.where(jnp.logical_and(inside_rows, inside_cols), source, -1)

        return choose

    return (
        one_hot(plane, plane, chooser(True, True, SHIFT_LAT, cols_here, SHIFT_LON)),
        one_hot(plane, SHIFT_LAT * own_cols, chooser(False, True, -SHIFT_LAT, own_cols, 0)),
        one_hot(plane, strip, chooser(True, False, 0, SHIFT_LON, -own_cols)),
        one_hot(plane, strip, chooser(False, False, -SHIFT_LAT, SHIFT_LON, -own_cols)),
    )


def strip_places(cols_here):
    own_cols = cols_here - SHIFT_LON
    plane = WLAT * cols_here
    strip = SHIFT_LAT * SHIFT_LON
    return (
        one_hot(SHIFT_LAT * own_cols, plane, lambda i: i // own_cols * cols_here + SHIFT_LON + i % own_cols),
        one_hot(strip, plane, lambda i: (i // SHIFT_LON + SHIFT_LAT) * cols_here + i % SHIFT_LON),
        one_hot(strip, plane, lambda i: i // SHIFT_LON * cols_here + i % SHIFT_LON),
    )


def lon_selectors():
    out = np.zeros((WLON, 3 * LANES, 2 * LANES), np.float32)
    for xj in range(WLON):
        for g in range(GROUPS):
            for xi in range(WLON):
                out[xj, g * SPAN + xi - xj + WLON - 1, g * WLON + xi] = 1
    return out


def dot(a, b, ca=1, cb=0):
    return lax.dot_general(a, b, (((ca,), (cb,)), ((), ())), preferred_element_type=F32)


def split(value):
    high = value.astype(BF)
    return high, (value - high.astype(F32)).astype(BF)


def prep_kernel(wx_far, gx_far, lat_out, lon_out, diag_out, wx_ref, gx_ref, sems):
    copies = [
        pltpu.make_async_copy(far, near, sems.at[i]) for i, (far, near) in enumerate(((wx_far, wx_ref), (gx_far, gx_ref)))
    ]
    for copy in copies:
        copy.start()
    picks = strip_places(wx_ref.shape[1] // WLAT)
    for copy in copies:
        copy.wait()
    for level in range(wx_ref.shape[0]):
        for pick, strip in zip(picks, (lat_out, lon_out, diag_out)):
            strip[level] = jnp.concatenate([dot(pick, ref[level]) for ref in (wx_ref, gx_ref)], axis=1).astype(BF)


def expand_kernel(last_ref, table_ref, sel_ref, bias_ref, flat_s, block_s, table_s):
    pairs, _, entries = table_ref.shape
    levs = pairs // HEADS
    for h in range(HEADS):
        for lev in range(levs):
            r = h * levs + lev
            flat_s[r : r + 1, :entries] = table_ref[lev * HEADS + h]
    for m in range(GROUPS):
        z_j, a_j = divmod(m, WLAT)
        for g in range(GROUPS):
            z_i, a_i = divmod(g, WLAT)
            at = SPAN * (((z_i * WLEV + z_j) * WLAT + a_i) * WLAT + a_j)
            block_s[m, :, g * SPAN : (g + 1) * SPAN] = flat_s[:pairs, at : at + SPAN]
        for j in range(3):
            table_s[j, pl.ds(m, pairs, stride=GROUPS), :] = block_s[m, :, j * LANES : (j + 1) * LANES]
    table = jnp.concatenate([table_s[j, :BIAS_ROWS] for j in range(3)], axis=1)[:, : GROUPS * SPAN]
    high, low = split(table)
    rows = levs * GROUPS
    row_id = lax.broadcasted_iota(jnp.int32, (BIAS_ROWS, TOK), 0)
    col_id = lax.broadcasted_iota(jnp.int32, (BIAS_ROWS, TOK), 1)
    m_j = row_id % GROUPS
    lev = row_id // GROUPS % levs
    a_i = col_id // WLON % WLAT
    z_i = col_id // (WLON * WLAT)
    cross_lev = jnp.logical_and(lev == levs - 1, m_j // WLAT != z_i)
    cross_lat = jnp.logical_and(last_ref[0] == 1, (m_j % WLAT >= SHIFT_LAT) != (a_i >= SHIFT_LAT))
    hide = jnp.where(jnp.logical_or(cross_lev, cross_lat), MASKED, 0.0)
    pad = jnp.zeros((rows, HLANES - HEADS * TOK), F32)
    for xj in range(WLON):
        sel = sel_ref[xj, : GROUPS * SPAN, :TOK]
        value = dot(high, sel) + dot(low, sel) + hide
        wide = jnp.concatenate([value[h * rows : (h + 1) * rows] for h in range(HEADS)] + [pad], axis=1)
        for t in range(HTILES):
            bias_ref[t, pl.ds(xj, rows, stride=WLON), :] = wide[:, t * LANES : (t + 1) * LANES]


def main_kernel(
    core_ref, wx_ref, gx_ref, lat_in, lon_in, diag_in, gain_ref, wqkv_ref, proj_ref,
    bias_hbm, sel_hbm,
    att_far, gi_far, keep_ref, send_ref,
    att_ref, gi_ref, x_s, g_s, normed_s, inv_s, q_s, k_s, v_s, da_s, dq_s, dk_s, dv_s, hid_t, dsum_s, pay_s, bias_s, sel_s, sems,
):
    bias_copy = pltpu.make_async_copy(bias_hbm, bias_s, sems.at[0])
    sel_copy = pltpu.make_async_copy(sel_hbm, sel_s, sems.at[1])
    bias_copy.start()
    sel_copy.start()
    levels = wx_ref.shape[0]
    half = TOK // 2
    windows = x_s.shape[0] // TOK
    place_own, *places = window_places(wx_ref.shape[1] // WLAT)
    for level in range(levels):
        back = (level + levels - 1) % levels
        k, z = back // WLEV, back % WLEV
        xw = dot(place_own, wx_ref[level])
        gw = dot(place_own, gx_ref[level])
        for place, strip in zip(places, (lat_in, lon_in, diag_in)):
            both = strip[level]
            xw = xw + dot(place, both[:, :CH])
            gw = gw + dot(place, both[:, CH:])
        for n in range(2):
            at = (2 * k + n) * TOK + z * half
            x_s[at : at + half, :] = xw[n * half : (n + 1) * half]
            g_s[at : at + half, :] = gw[n * half : (n + 1) * half]

    gain = gain_ref[...]
    inv_root = HD ** (-0.5)

    def eye(n):
        return (lax.broadcasted_iota(jnp.int32, (n, n), 0) == lax.broadcasted_iota(jnp.int32, (n, n), 1)).astype(F32).astype(BF)

    eye_c = eye(CH)
    eye_t = eye(TOK)
    chunks = [slice(at, at + CHUNK) for at in range(0, x_s.shape[0], CHUNK)]
    for rows in chunks:
        x = x_s[rows]
        centred = x - jnp.mean(x, axis=-1, keepdims=True)
        inv_std = lax.rsqrt(jnp.mean(centred * centred, axis=-1, keepdims=True) + EPSILON)
        normed = centred * inv_std
        normed_s[rows] = normed
        inv_s[rows] = jnp.broadcast_to(inv_std, (CHUNK, LANES))
        hidden = (normed * gain).astype(BF)
        q_s[rows] = (dot(hidden, wqkv_ref[0]) * inv_root).astype(BF)
        k_s[rows] = dot(hidden, wqkv_ref[1]).astype(BF)
        v_s[rows] = dot(hidden, wqkv_ref[2]).astype(BF)
        da_s[rows] = dot(g_s[rows].astype(BF), proj_ref[...], 1, 1).astype(BF)
        hid_t[:, rows] = dot(eye_c, hidden, 1, 1).astype(BF)

    channel = lax.broadcasted_iota(jnp.int32, (TOK, CH), 1)
    head_mask = [jnp.logical_and(channel >= h * HD, channel < (h + 1) * HD) for h in range(HEADS)]
    zero = jnp.zeros((TOK, CH), BF)
    tail = jnp.zeros((HLANES - HEADS * TOK, CH), BF)

    def per_head(value):
        return jnp.concatenate([jnp.where(mask, value, zero) for mask in head_mask] + [tail], axis=0)

    bias_copy.wait()
    gproj = jnp.zeros((CH, CH), F32)
    for w in range(windows):
        rows = slice(w * TOK, (w + 1) * TOK)
        first = w % 2 == 0
        lev_rows = slice(w // 2 * TOK, (w // 2 + 1) * TOK)
        key, v = k_s[rows], v_s[rows]
        q_heads = per_head(q_s[rows])
        da_heads = per_head(da_s[rows])
        key_t = dot(eye_c, key, 1, 1).astype(BF)
        v_t = dot(eye_c, v, 1, 1).astype(BF)
        scores = dot(key, q_heads, 1, 1)
        scores = scores + jnp.concatenate([bias_s[t, lev_rows, :] for t in range(HTILES)], axis=1)
        dp = dot(v, da_heads, 1, 1)
        e = jnp.exp(scores - jnp.max(scores, axis=0, keepdims=True))
        probs = (e * (1.0 / jnp.sum(e, axis=0, keepdims=True))).astype(BF)
        dv_s[rows] = dot(probs, da_heads).astype(BF)
        pf = probs.astype(F32)
        t_prod = pf * dp
        ds = t_prod - pf * jnp.sum(t_prod, axis=0, keepdims=True)
        dsb = ds.astype(BF)
        for t in range(HTILES):
            part = ds[:, t * LANES : (t + 1) * LANES]
            dsum_s[t, lev_rows, :] = part if first else dsum_s[t, lev_rows, :] + part
        dk_s[rows] = dot(dsb, q_heads).astype(BF)
        att_t = jnp.concatenate(
            [dot(v_t[h * HD : (h + 1) * HD], probs[:, h * TOK : (h + 1) * TOK]) for h in range(HEADS)], axis=0
        ).astype(BF)
        dq_t = jnp.concatenate(
            [dot(key_t[h * HD : (h + 1) * HD], dsb[:, h * TOK : (h + 1) * TOK]) for h in range(HEADS)], axis=0
        )
        dq_t = (dq_t * inv_root).astype(BF)
        att_ref[rows] = dot(eye_t, att_t, 1, 1).astype(BF)
        dq_s[rows] = dot(eye_t, dq_t, 1, 1).astype(BF)
        gproj = gproj + dot(att_t, g_s[rows].astype(BF))

    att_copy = pltpu.make_async_copy(att_ref, att_far, sems.at[2])
    att_copy.start()
    g_gain = jnp.zeros((1, CH), F32)
    for rows in chunks:
        gh = (
            dot(dq_s[rows], wqkv_ref[0], 1, 1)
            + dot(dk_s[rows], wqkv_ref[1], 1, 1)
            + dot(dv_s[rows], wqkv_ref[2], 1, 1)
        )
        normed = normed_s[rows]
        g_gain = g_gain + jnp.sum(gh * normed, axis=0, keepdims=True)
        gn = gh * gain
        gi = inv_s[rows][:, :1] * (
            gn
            - jnp.mean(gn, axis=-1, keepdims=True)
            - normed * jnp.mean(gn * normed, axis=-1, keepdims=True)
        )
        gi_ref[rows] = gi.astype(BF)

    gi_copy = pltpu.make_async_copy(gi_ref, gi_far, sems.at[3])
    gi_copy.start()
    g_wide = [dot(hid_t[...], part[...]) for part in (dq_s, dk_s, dv_s)]
    weights = jnp.concatenate(g_wide + [gproj], axis=1)
    for j in range(WTILES):
        pay_s[j * CH : (j + 1) * CH, :] = weights[:, j * LANES : (j + 1) * LANES]
    pay_s[GROW:, :] = jnp.zeros((PAY - GROW, LANES), F32)
    pay_s[GROW : GROW + 1, :] = g_gain[:, :LANES]
    pay_s[GROW + 1 : GROW + 2, : CH - LANES] = g_gain[:, LANES:]

    sel_copy.wait()
    lev_groups = BIAS_ROWS // HEADS
    g_bias = jnp.zeros((BIAS_ROWS, 3 * LANES), F32)
    for xj in range(WLON):
        wide = jnp.concatenate(
            [dsum_s[t, pl.ds(xj, lev_groups, stride=WLON), :] for t in range(HTILES)], axis=1
        ).astype(BF)
        stacked = jnp.concatenate([wide[:, h * TOK : (h + 1) * TOK] for h in range(HEADS)], axis=0)
        g_bias = g_bias + dot(stacked, sel_s[xj, :, :TOK], 1, 1)
    for j in range(3):
        pay_s[BROW + j * BIAS_ROWS : BROW + (j + 1) * BIAS_ROWS, :] = g_bias[:, j * LANES : (j + 1) * LANES]
    core = core_ref[0]
    half_rows = PAY // 2
    keep_ref[...] = pay_s[pl.ds(pl.multiple_of(core * half_rows, half_rows), half_rows), :].astype(BF)
    send_ref[...] = pay_s[pl.ds(pl.multiple_of((1 - core) * half_rows, half_rows), half_rows), :].astype(BF)
    att_copy.wait()
    gi_copy.wait()


def return_kernel(
    wx_ref, gx_ref, att_ref, gi_ref, proj_ref,
    base_ref, gbase_ref, lat_out, lon_out, diag_out, br_s, gi_s,
):
    br_s[...] = dot(att_ref[...], proj_ref[...])
    gi_s[...] = gi_ref[...].astype(F32)
    place_own, *places = window_places(wx_ref.shape[1] // WLAT)
    levels = wx_ref.shape[0]
    half = TOK // 2
    for level in range(levels):
        back = (level + levels - 1) % levels
        k, z = back // WLEV, back % WLEV
        moved = []
        for src, own_in, own_out in ((br_s, wx_ref, base_ref), (gi_s, gx_ref, gbase_ref)):
            starts = [(2 * k + n) * TOK + z * half for n in range(2)]
            rows = jnp.concatenate([src[at : at + half, :] for at in starts], axis=0).astype(BF)
            own_out[level] = (own_in[level].astype(F32) + dot(place_own, rows, 0, 0)).astype(BF)
            moved.append(rows)
        for place, strip in zip(places, (lat_out, lon_out, diag_out)):
            strip[level] = jnp.concatenate(
                [dot(place, rows, 0, 0) for rows in moved], axis=1
            ).astype(BF)


def add_kernel(base_ref, gbase_ref, lat_in, lon_in, diag_in, out_ref, gout_ref):
    picks = strip_places(base_ref.shape[1] // WLAT)
    for level in range(base_ref.shape[0]):
        up = base_ref[level].astype(F32)
        gup = gbase_ref[level].astype(F32)
        for pick, strip in zip(picks, (lat_in, lon_in, diag_in)):
            both = strip[level]
            up = up + dot(pick, both[:, :CH], 0, 0)
            gup = gup + dot(pick, both[:, CH:], 0, 0)
        out_ref[level] = up.astype(BF)
        gout_ref[level] = gup.astype(BF)


def finish_kernel(
    factor, core_ref, mine_ref, other_ref, gqkv_ref, gproj_ref, ggain_ref, gbias_ref, full_s, table_s,
):
    core = core_ref[0]
    half_rows = PAY // 2
    full_s[pl.ds(pl.multiple_of(core * half_rows, half_rows), half_rows), :] = mine_ref[...].astype(F32) * factor
    full_s[pl.ds(pl.multiple_of((1 - core) * half_rows, half_rows), half_rows), :] = other_ref[...].astype(F32) * factor
    tiles = [full_s[j * CH : (j + 1) * CH, :] for j in range(WTILES)]
    for j in range(4):
        gqkv_ref[:, j * LANES : (j + 1) * LANES] = tiles[j]
    cut = 3 * CH - 4 * LANES
    gqkv_ref[:, 4 * LANES :] = tiles[4][:, :cut]
    gproj_ref[...] = jnp.concatenate([tiles[4][:, cut:], tiles[5]], axis=1)
    ggain_ref[...] = jnp.concatenate(
        [full_s[GROW : GROW + 1, :], full_s[GROW + 1 : GROW + 2, : CH - LANES]], axis=1
    )
    pairs = BIAS_ROWS // GROUPS
    levs = pairs // HEADS
    for m in range(GROUPS):
        z_j, a_j = divmod(m, WLAT)
        block = jnp.concatenate(
            [full_s[pl.ds(BROW + j * BIAS_ROWS + m, pairs, stride=GROUPS), :] for j in range(3)], axis=1
        )
        for g in range(GROUPS):
            z_i, a_i = divmod(g, WLAT)
            to = SPAN * (((z_i * WLEV + z_j) * WLAT + a_i) * WLAT + a_j)
            table_s[:pairs, to : to + SPAN] = block[:, g * SPAN : (g + 1) * SPAN]
    for h in range(HEADS):
        for lev in range(levs):
            r = h * levs + lev
            gbias_ref[lev * HEADS + h] = table_s[r : r + 1, : gbias_ref.shape[2]]


def passed(value, lat_step, lon_step):
    lats, highs, zs = lax.axis_size("lat"), lax.axis_size("yhi"), lax.axis_size("z")
    lons = highs * zs
    pairs = [
        (b * lats + a, (b + lon_step) % lons * lats + (a + lat_step) % lats)
        for b in range(lons)
        for a in range(lats)
    ]
    return lax.ppermute(value, ("yhi", "z", "lat"), pairs)


def swapped(value):
    return lax.ppermute(value, "core", [(0, 1), (1, 0)])


def total_over_devices(keep, send, between, last):
    wide = ("ylo", "yhi", "z")
    peers = lax.axis_size("ylo") * lax.axis_size("yhi") * lax.axis_size("z")
    half = (keep.astype(F32) + swapped(send).astype(F32)).astype(BF)
    inputs, fn = between
    half, inputs = lax.optimization_barrier((half, inputs))
    pieces = lax.all_to_all(half, wide, 0, 0, tiled=True)
    keeps, strips = fn(inputs)
    pieces, _ = lax.optimization_barrier((pieces, strips))
    backs = [passed(strip, *step) for strip, step in zip(strips, ((1, 0), (0, 1), (1, 1)))]
    piece = jnp.sum(pieces.reshape(peers, PIECE, LANES).astype(F32), axis=0)
    lats = lax.axis_size("lat")
    place_here = lax.axis_index("core") * peers + lax.axis_index(wide)
    shared = jnp.logical_or(place_here < BROW // PIECE, place_here >= GROW // PIECE)
    others = [
        lax.ppermute(piece, "lat", [(a, (a + step) % lats) for a in range(lats)]) for step in range(1, lats)
    ]
    others, backs = lax.optimization_barrier((others, tuple(backs)))
    others = sum(others)
    piece = jnp.where(shared, piece + others, piece).astype(BF)
    spread = jnp.broadcast_to(piece[None], (peers, PIECE, LANES)).reshape(half.shape)
    spread, backs = lax.optimization_barrier((spread, backs))
    mine = lax.all_to_all(spread, wide, 0, 0, tiled=True)
    mine, outs = lax.optimization_barrier((mine, last(*keeps, *backs)))
    return mine, swapped(mine), outs


def call(kernel, out_shape, scratch=(), smem=0, count=0, flops=0, far=0, room=12, far_out=()):
    specs = [pl.BlockSpec(memory_space=pltpu.SMEM)] * smem
    specs += [pl.BlockSpec(memory_space=pltpu.VMEM)] * (count - smem - far)
    specs += [pl.BlockSpec(memory_space=pl.ANY)] * far
    return pl.pallas_call(
        kernel,
        out_shape=out_shape,
        in_specs=specs,
        out_specs=jax.tree.unflatten(
            jax.tree.structure(out_shape),
            [
                pl.BlockSpec(memory_space=pl.ANY if i in far_out else pltpu.VMEM)
                for i in range(len(jax.tree.leaves(out_shape)))
            ],
        ),
        scratch_shapes=list(scratch),
        compiler_params=pltpu.CompilerParams(vmem_limit_bytes=room * MIB),
        cost_estimate=pl.CostEstimate(flops=flops, bytes_accessed=flops // 500, transcendentals=0),
    )


def sds(shape, dtype):
    return jax.ShapeDtypeStruct(shape, dtype)


def shards(weather, cotangent, norm_gain, qkv_weight, proj_weight, bias_table):
    samples, levels, rows_here, cols_here, channels = weather.shape
    lat_index = lax.axis_index("lat")
    lat_count = lax.axis_size("lat")
    plane = rows_here * cols_here
    own_cols = cols_here - SHIFT_LON
    wx = weather.reshape(levels, plane, CH)
    gx = cotangent.reshape(levels, plane, CH)
    edge = SHIFT_LAT * SHIFT_LON
    lat_shape = sds((levels, SHIFT_LAT * own_cols, 2 * CH), BF)
    edge_shape = sds((levels, edge, 2 * CH), BF)
    near = [pltpu.VMEM((levels, plane, CH), BF)] * 2
    strips = call(
        prep_kernel, (lat_shape, edge_shape, edge_shape), scratch=near + [pltpu.SemaphoreType.DMA((2,))],
        count=2, far=2, flops=10**9,
    )(*[pltpu.with_memory_space_constraint(v, pltpu.HBM) for v in (wx, gx)])
    lat_in = passed(strips[0], -1, 0)
    lon_in = passed(strips[1], 0, -1)
    diag_in = passed(strips[2], -1, -1)

    lev_windows = bias_table.shape[0]
    pairs = lev_windows * HEADS
    entries = bias_table.shape[-1]
    table = bias_table.transpose(0, 2, 1, 3).reshape(pairs, 1, entries)
    last = (lat_index == lat_count - 1).astype(jnp.int32).reshape(1)
    sel = jnp.asarray(lon_selectors(), BF)
    bias_rows = lev_windows * TOK
    flat_shape = pltpu.VMEM((pairs + SPARE, -(-entries // LANES) * LANES), F32)
    bias_shape = (HTILES, bias_rows + SPARE, LANES)
    bias = call(
        expand_kernel,
        sds(bias_shape, F32),
        scratch=[flat_shape, pltpu.VMEM((GROUPS, pairs, 3 * LANES), F32), pltpu.VMEM((3, BIAS_ROWS + SPARE, LANES), F32)],
        smem=1, count=3, flops=10**9,
    )(last, table, sel)

    wqkv = qkv_weight.reshape(CH, 3, CH).transpose(1, 0, 2)
    tokens = levels * plane
    plane_shape = sds((levels, plane, CH), BF)
    token_shape = sds((tokens, CH), BF)
    core = lax.axis_index("core").astype(jnp.int32).reshape(1)
    half_shape = sds((PAY // 2, LANES), BF)
    wide_f = pltpu.VMEM((tokens, CH), F32)
    wide_b = pltpu.VMEM((tokens, CH), BF)
    att, gi, keep, send = call(
        main_kernel,
        (pltpu.HBM(token_shape.shape, BF), pltpu.HBM(token_shape.shape, BF), half_shape, half_shape),
        scratch=[wide_b, wide_b, wide_f, wide_f, wide_f, pltpu.VMEM((tokens, LANES), F32)]
        + [wide_b] * 7
        + [
            pltpu.VMEM((CH, tokens), BF),
            pltpu.VMEM(bias_shape, F32),
            pltpu.VMEM((PAY, LANES), F32),
            pltpu.VMEM(bias_shape, F32),
            pltpu.VMEM(sel.shape, BF),
            pltpu.SemaphoreType.DMA((4,)),
        ],
        smem=1,
        count=11,
        far=2,
        far_out=(0, 1),
        flops=10**10,
        room=28,
    )(core, wx, gx, lat_in, lon_in, diag_in, norm_gain.reshape(1, CH), wqkv, proj_weight, bias, sel)

    def give_back(inputs):
        base, gbase, *strips = call(
            return_kernel,
            (plane_shape, plane_shape, lat_shape, edge_shape, edge_shape),
            scratch=[wide_f, wide_f],
            count=5,
            flops=2 * 10**9,
            room=56,
        )(wx, gx, *inputs, proj_weight)
        return (base, gbase), strips

    def add_up(*parts):
        return call(add_kernel, (plane_shape, plane_shape), count=5, flops=2 * 10**9)(*parts)

    mine, other, (out, gout) = total_over_devices(keep, send, ((att, gi), give_back), add_up)
    factor = (samples * levels * rows_here * cols_here * lax.axis_size(("ylo", "core", "yhi", "z", "lat"))) ** (-0.5)
    gqkv, gproj, ggain, gbias = call(
        functools.partial(finish_kernel, factor),
        (sds(qkv_weight.shape, F32), sds(proj_weight.shape, F32), sds((1, CH), F32), sds((pairs, 1, entries), F32)),
        scratch=[pltpu.VMEM((PAY, LANES), F32), flat_shape],
        smem=1,
        count=3,
        flops=10**9,
    )(core, mine, other)
    return (
        out.reshape(weather.shape),
        gout.reshape(weather.shape),
        gqkv,
        gproj,
        ggain.reshape(CH),
        gbias.reshape(lev_windows, HEADS, 1, entries).transpose(0, 2, 1, 3),
    )


def solution(mesh):
    fine = jax.sharding.Mesh(mesh.devices.reshape(2, 2, 2, 8, 4), ("ylo", "core", "yhi", "z", "lat"))
    dp, lon = ("ylo", "core"), ("yhi", "z")
    grid = P(dp, None, "lat", lon, None)
    table = P(None, "lat", None, None)
    return jax.shard_map(
        shards,
        mesh=fine,
        in_specs=(grid, grid, P(), P(), P(), table),
        out_specs=(grid, grid, P(), P(), P(), table),
        check_vma=False,
    )
```
